128 devices in a mesh: ctx: 32 (over x, z_lo, y), wshard: 4 (over z_hi, core).
Axes of the slice: x: 4, y: 4, z: 4 (z_hi: 2, z_lo: 2; z = z_hi * 2 + z_lo), core: 2. Of those that a mesh axis runs over, the one named last changes fastest.
Arguments:
- pixels: bfloat16 [4, 16384, 261], P('wshard', 'ctx'), may hold values from -6 to 6
- latents: bfloat16 [4, 512, 1024], P('wshard', 'ctx'), may hold values from -6 to 6
- input_segments: int32 [4, 16384], P('wshard', 'ctx'), may hold values from 0 to 3, as said below
- latent_offsets: int32 [4, 4], P('wshard'), may hold values from 0 to 511, as said below
- pixel_gain: bfloat16 [261], replicated, may hold values from 0.5 to 1.5
- pixel_shift: bfloat16 [261], replicated, may hold values from -1.5 to 1.5
- query_weight: bfloat16 [1024, 1024], P(None, 'wshard'), may hold values from -0.1875 to 0.1875
- key_weight: bfloat16 [261, 1024], P(None, 'wshard'), may hold values from -0.375 to 0.375
- value_weight: bfloat16 [261, 1024], P(None, 'wshard'), may hold values from -0.375 to 0.375
- cross_output: bfloat16 [1024, 1024], P(None, 'wshard'), may hold values from -3 to 3
- cross_up: bfloat16 [1024, 1024], P(None, 'wshard'), may hold values from -0.1875 to 0.1875
- cross_down: bfloat16 [1024, 1024], P(None, 'wshard'), may hold values from -0.1875 to 0.1875
- self_projection: bfloat16 [1024, 3072], P(None, 'wshard'), may hold values from -0.1875 to 0.1875
- self_output: bfloat16 [1024, 1024], P(None, 'wshard'), may hold values from -1.5 to 1.5
- self_up: bfloat16 [1024, 1024], P(None, 'wshard'), may hold values from -0.1875 to 0.1875
- self_down: bfloat16 [1024, 1024], P(None, 'wshard'), may hold values from -0.1875 to 0.1875
- norm_gains: bfloat16 [4, 1024], P(None, 'wshard'), may hold values from 0.5 to 1.5
- norm_shifts: bfloat16 [4, 1024], P(None, 'wshard'), may hold values from -1.5 to 1.5
- dense_bias: bfloat16 [4, 1024], P(None, 'wshard'), may hold values from -1.5 to 1.5
- cotangent: bfloat16 [4, 512, 1024], P('wshard', 'ctx'), may hold values from -6 to 6
Outputs:
- latents_out: bfloat16 [4, 512, 1024], P('wshard', 'ctx')
- latent_grad: bfloat16 [4, 512, 1024], P('wshard', 'ctx')
- pixel_grad: bfloat16 [4, 16384, 261], P('wshard', 'ctx')
- pixel_gain_grad: float32 [261], replicated
- pixel_shift_grad: float32 [261], replicated
- query_weight_grad: float32 [1024, 1024], P(None, 'wshard')
- key_weight_grad: float32 [261, 1024], P(None, 'wshard')
- value_weight_grad: float32 [261, 1024], P(None, 'wshard')
- cross_output_grad: float32 [1024, 1024], P(None, 'wshard')
- cross_up_grad: float32 [1024, 1024], P(None, 'wshard')
- cross_down_grad: float32 [1024, 1024], P(None, 'wshard')
- self_projection_grad: float32 [1024, 3072], P(None, 'wshard')
- self_output_grad: float32 [1024, 1024], P(None, 'wshard')
- self_up_grad: float32 [1024, 1024], P(None, 'wshard')
- self_down_grad: float32 [1024, 1024], P(None, 'wshard')
- norm_gains_grad: float32 [4, 1024], P(None, 'wshard')
- norm_shifts_grad: float32 [4, 1024], P(None, 'wshard')
- dense_bias_grad: float32 [4, 1024], P(None, 'wshard')
The draws below stay inside these ranges and needn't reach their ends.
Inputs may be any that keep to these rules, and one draw needn't show every extreme that they name: `input_segments`: within each sequence the document numbers never fall and every one of the 4 documents has one or more pixel rows; one document, drawn from the seed, has rows on every index of ctx. `latent_offsets`: each row rises strictly from 0; every document has one or more latents, the same document as in input_segments has latents on every index of ctx.
All inputs are finite; a program needn't handle non-finite values.
Results may differ from the reference program's by a relative error of at most 0.025.
Values may be sent and summed in bfloat16 or wider, within the bound.
No kernel may reach another device: no remote copies, remote signals or barrier semaphores. Data moves between devices by JAX's collectives and lax.ppermute only.
A program may use at most 384 MiB of HBM per device.

```python
import jax
import jax.numpy as jnp
from jax import lax

D = 1024
C = 261
HEADS = 8
ROWS_DEV = 512
LAT_DEV = 16
DOCS = 4
GROUPS = 4
GROUP_ROWS = 16384
GROUP_LAT = 512


def largest_doc(key):
    return jax.random.randint(jax.random.fold_in(key, 11), (GROUPS,), 0, DOCS)


def doc_lengths(key, largest, per_device, whole_count):
    smaller = jax.random.randint(key, (GROUPS, DOCS), 1, per_device // DOCS + 1)
    chosen = jnp.arange(DOCS)[None, :] == largest[:, None]
    others = jnp.sum(jnp.where(chosen, 0, smaller), 1, keepdims=True)
    return jnp.where(chosen, whole_count - others, smaller).astype(jnp.int32)


def draw_input_segments(key, part):
    largest = largest_doc(key)
    lengths = doc_lengths(jax.random.fold_in(key, 21), largest, ROWS_DEV, GROUP_ROWS)
    doc_ends = jnp.cumsum(lengths, 1)
    position = jnp.arange(GROUP_ROWS, dtype=jnp.int32)
    return jnp.sum((doc_ends[:, None, :] <= position[None, :, None]).astype(jnp.int32), 2)


def draw_latent_offsets(key, part):
    largest = largest_doc(key)
    lengths = doc_lengths(jax.random.fold_in(key, 31), largest, LAT_DEV, GROUP_LAT)
    return (jnp.cumsum(lengths, 1) - lengths).astype(jnp.int32)


def levels(rng, extent, pieces, smallest, high):
    level = 1.0
    for dim, shards_of in pieces:
        heights = jax.random.uniform(jax.random.fold_in(jax.random.fold_in(rng, 6), dim), (shards_of,), jnp.float32, smallest / len(pieces), high / len(pieces))
        level = level * jnp.repeat(jnp.exp(heights), extent[dim] // shards_of).reshape((-1,) + (1,) * (len(extent) - 1 - dim))
    return level


def noise(rng, dims, spread, bound, pieces=(), held_as=jnp.bfloat16):
    drawn = jax.random.normal(rng, dims, jnp.float32) * spread
    if len(pieces) > 0:
        drawn = levels(rng, dims, pieces, -0.22, 0.18) * drawn
    return jnp.clip(drawn, min=-bound, max=bound).astype(held_as)


def setup_inputs(seed: int = 0) -> dict:
    seeds = jax.random.split(jax.random.key(seed), 21)
    pixels = noise(seeds[0], (GROUPS, GROUP_ROWS, C), 1.0, 6.0, ((0, 4), (1, 32)))
    latents = noise(seeds[1], (GROUPS, GROUP_LAT, D), 1.0, 6.0, ((0, 4), (1, 32)))
    input_segments = draw_input_segments(jax.random.fold_in(seeds[20], 71), 0)
    latent_offsets = draw_latent_offsets(jax.random.fold_in(seeds[20], 71), 0)
    pixel_gain = jnp.clip(1.0 + 0.1 * jax.random.normal(seeds[4], (C,), jnp.float32), 0.5, 1.5).astype(jnp.bfloat16)
    pixel_shift = noise(seeds[5], (C,), 0.3, 1.5)
    query_weight = noise(seeds[6], (D, D), D ** -0.5, 0.1875, ((1, 4),))
    key_weight = noise(seeds[7], (C, D), C ** -0.5, 0.375, ((1, 4),))
    value_weight = noise(seeds[8], (C, D), C ** -0.5, 0.375, ((1, 4),))
    cross_output = noise(seeds[9], (D, D), 4 ** -0.5, 3.0, ((1, 4),))
    cross_up = noise(seeds[10], (D, D), D ** -0.5, 0.1875, ((1, 4),))
    cross_down = noise(seeds[11], (D, D), D ** -0.5, 0.1875, ((1, 4),))
    self_projection = noise(seeds[12], (D, 3 * D), D ** -0.5, 0.1875, ((1, 4),))
    self_output = noise(seeds[13], (D, D), 16 ** -0.5, 1.5, ((1, 4),))
    self_up = noise(seeds[14], (D, D), D ** -0.5, 0.1875, ((1, 4),))
    self_down = noise(seeds[15], (D, D), D ** -0.5, 0.1875, ((1, 4),))
    norm_gains = jnp.clip(1.0 + 0.1 * jax.random.normal(seeds[16], (4, D), jnp.float32), 0.5, 1.5).astype(jnp.bfloat16)
    norm_shifts = noise(seeds[17], (4, D), 0.3, 1.5, ((1, 4),))
    dense_bias = noise(seeds[18], (4, D), 0.3, 1.5, ((1, 4),))
    cotangent = noise(seeds[19], (GROUPS, GROUP_LAT, D), 1.0, 6.0, ((0, 4), (1, 32)))
    return {"pixels": pixels, "latents": latents, "input_segments": input_segments, "latent_offsets": latent_offsets, "pixel_gain": pixel_gain, "pixel_shift": pixel_shift, "query_weight": query_weight, "key_weight": key_weight, "value_weight": value_weight, "cross_output": cross_output, "cross_up": cross_up, "cross_down": cross_down, "self_projection": self_projection, "self_output": self_output, "self_up": self_up, "self_down": self_down, "norm_gains": norm_gains, "norm_shifts": norm_shifts, "dense_bias": dense_bias, "cotangent": cotangent}


@jax.custom_vjp
def low(v):
    return lax.optimization_barrier(v.astype(jnp.bfloat16)).astype(jnp.float32)

@jax.custom_vjp
def low_back(v):
    return v

def low_keep(v):
    return (low(v), None)

def low_pass(kept, grad):
    return (grad,)

def back_keep(v):
    return (v, None)

def back_low(kept, grad):
    return (low(grad),)
low.defvjp(low_keep, low_pass)
low_back.defvjp(back_keep, back_low)
highest = lax.Precision.HIGHEST

def matmul(left, right):
    return jnp.dot(left, right, precision=highest)

def norm_rows(stream, gain, shift):
    center = lax.optimization_barrier(jnp.mean(stream, -1, keepdims=True))
    centred = stream - center
    variance = lax.optimization_barrier(jnp.mean(centred * centred, -1, keepdims=True))
    return centred * lax.rsqrt(variance + 1e-05) * gain + shift

def masked_softmax(scores, same_doc):
    masked = jnp.where(same_doc, scores, -1e+30)
    row_top = lax.optimization_barrier(jnp.max(masked, -1, keepdims=True))
    weights = jnp.exp(masked - row_top)
    return weights / lax.optimization_barrier(jnp.sum(weights, -1, keepdims=True))

def latent_ids(offsets, count):
    position = jnp.arange(count)
    return lax.optimization_barrier(jnp.sum((offsets[None, 1:] <= position[:, None]).astype(jnp.int32), 1))

def feed_forward(stream, gain, shift, w_inner, b_inner, w_outer, b_outer):
    normed = low(norm_rows(stream, gain, shift))
    pre_act = low_back(matmul(normed, w_inner) + b_inner)
    activ = low(jax.nn.gelu(pre_act))
    return low_back(matmul(activ, w_outer) + b_outer)

def group_forward(params, pixel_rows, latent_rows, segments, offsets):
    pixel_gain, pixel_shift, query_weight, key_weight, value_weight, cross_output, cross_up, cross_down, self_projection, self_output, self_up, self_down, norm_gains, norm_shifts, dense_bias = params
    width = latent_rows.shape[1]
    heads = HEADS
    head_dim = width // heads
    lat_count = latent_rows.shape[0]
    lat_ids = latent_ids(offsets, lat_count)
    pixel_low = low(norm_rows(pixel_rows, pixel_gain, pixel_shift))
    cross_low = low(norm_rows(latent_rows, norm_gains[0], norm_shifts[0]))
    query = low(low_back(matmul(cross_low, query_weight)))
    keys = low(matmul(pixel_low, key_weight))
    values = low(matmul(pixel_low, value_weight))
    same_cross = lat_ids[:, None] == segments[None, :]
    cross_scores = low_back(matmul(query, keys.T) * width ** (-0.5))
    cross_probs = low(masked_softmax(cross_scores, same_cross))
    attended = low(low_back(matmul(cross_probs, values)))
    latent_one = latent_rows + low_back(matmul(attended, cross_output))
    latent_two = latent_one + feed_forward(latent_one, norm_gains[1], norm_shifts[1], cross_up, dense_bias[0], cross_down, dense_bias[1])
    self_low = low(norm_rows(latent_two, norm_gains[2], norm_shifts[2]))
    triple = low(low_back(matmul(self_low, self_projection)))
    self_query = triple[:, :width].reshape(lat_count, heads, head_dim)
    self_keys = triple[:, width:2 * width].reshape(lat_count, heads, head_dim)
    self_values = triple[:, 2 * width:].reshape(lat_count, heads, head_dim)
    same_self = (lat_ids[:, None] == lat_ids[None, :])[None]
    self_scores = low_back(jnp.einsum('qhd,khd->hqk', self_query, self_keys, precision=highest) * head_dim ** (-0.5))
    self_probs = low(masked_softmax(self_scores, same_self))
    self_att = low(low_back(jnp.einsum('hqk,khd->qhd', self_probs, self_values, precision=highest).reshape(lat_count, width)))
    latent_three = latent_two + low_back(matmul(self_att, self_output))
    return latent_three + feed_forward(latent_three, norm_gains[3], norm_shifts[3], self_up, dense_bias[2], self_down, dense_bias[3])

def reference(pixels, latents, input_segments, latent_offsets, pixel_gain, pixel_shift, query_weight, key_weight, value_weight, cross_output, cross_up, cross_down, self_projection, self_output, self_up, self_down, norm_gains, norm_shifts, dense_bias, cotangent):
    params = tuple((item.astype(jnp.float32) for item in (pixel_gain, pixel_shift, query_weight, key_weight, value_weight, cross_output, cross_up, cross_down, self_projection, self_output, self_up, self_down, norm_gains, norm_shifts, dense_bias)))

    def total(param_set, pixel_all, latent_all):

        def single(item):
            return group_forward(param_set, item[0], item[1], item[2], item[3])
        return lax.map(jax.checkpoint(single), (pixel_all, latent_all, input_segments, latent_offsets))
    result, pull = jax.vjp(total, params, pixels.astype(jnp.float32), latents.astype(jnp.float32))
    param_grads, pixel_grads, latent_grads = pull(cotangent.astype(jnp.float32))
    return (result.astype(jnp.bfloat16), latent_grads.astype(jnp.bfloat16), pixel_grads.astype(jnp.bfloat16), param_grads[0], param_grads[1], param_grads[2], param_grads[3], param_grads[4], param_grads[5], param_grads[6], param_grads[7], param_grads[8], param_grads[9], param_grads[10], param_grads[11], param_grads[12], param_grads[13], param_grads[14])
```

```python
import jax
import jax.numpy as jnp
from jax import lax
from jax.sharding import Mesh, PartitionSpec as P

HEADS = 8
CTX = ("x", "zl", "y")
SHARD = ("zh", "core")
BF = jnp.bfloat16
F32 = jnp.float32


def mm(left, right):
    return lax.dot_general(left, right, (((1,), (0,)), ((), ())), preferred_element_type=F32)


def mm_t(left, right):
    return lax.dot_general(left, right, (((1,), (1,)), ((), ())), preferred_element_type=F32)


def t_mm(left, right):
    return lax.dot_general(left, right, (((0,), (0,)), ((), ())), preferred_element_type=F32)


def shift(value, axis, by):
    count = lax.axis_size(axis)
    return lax.ppermute(value, axis, [(i, (i + by) % count) for i in range(count)])


def facing(value):
    return lax.ppermute(value, ("zl", "zh"), [(i, 3 - i) for i in range(4)])


def spread(rows):
    return lax.all_to_all(jnp.tile(rows, (32, 1)), CTX, 0, 0, tiled=True)


def put(whole, part, row, column):
    return lax.dynamic_update_slice(whole, part, (row, column))


def gather_shards(own):
    n, width = own.shape
    piece = n // 8
    ix, iy = lax.axis_index("x"), lax.axis_index("y")
    zh, core = lax.axis_index("zh"), lax.axis_index("core")
    first = lax.dynamic_slice(own, (ix * piece, 0), (piece, width))
    second = lax.dynamic_slice(own, (n // 2 + iy * piece, 0), (piece, width))
    first, second = facing(first), facing(second)
    other = jnp.zeros_like(own)
    other = put(other, first, ix * piece, 0)
    other = put(other, second, n // 2 + iy * piece, 0)
    for by in (1, 2, 3):
        other = put(other, shift(first, "x", by), (ix + 4 - by) % 4 * piece, 0)
        other = put(other, shift(second, "y", by), n // 2 + (iy + 4 - by) % 4 * piece, 0)
    own_there, other_there = shift(own, "core", 1), shift(other, "core", 1)
    whole = jnp.zeros((n, 4 * width), own.dtype)
    whole = put(whole, own, 0, (zh * 2 + core) * width)
    whole = put(whole, own_there, 0, (zh * 2 + 1 - core) * width)
    whole = put(whole, other, 0, ((1 - zh) * 2 + core) * width)
    whole = put(whole, other_there, 0, ((1 - zh) * 2 + 1 - core) * width)
    return whole


def in_three(value):
    high = lax.reduce_precision(value, 8, 7)
    rest = value - high
    middle = lax.reduce_precision(rest, 8, 7)
    return high.astype(BF), middle.astype(BF), (rest - middle).astype(BF)


def norm_rows(stream, gain, bias):
    center = jnp.mean(stream, -1, keepdims=True)
    centred = stream - center
    variance = jnp.mean(centred * centred, -1, keepdims=True)
    return centred * lax.rsqrt(variance + 1e-05) * gain + bias


def norm_back(stream, gain, grad):
    center = jnp.mean(stream, -1, keepdims=True)
    centred = stream - center
    variance = jnp.mean(centred * centred, -1, keepdims=True)
    scale = lax.rsqrt(variance + 1e-05)
    hat = centred * scale
    hat_grad = grad * gain
    back = scale * (
        hat_grad
        - jnp.mean(hat_grad, -1, keepdims=True)
        - hat * jnp.mean(hat_grad * hat, -1, keepdims=True)
    )
    return back, jnp.sum(grad * hat, 0), jnp.sum(grad, 0)


def dense_forward(stream, gain, bias, w_inner, b_inner, w_outer, b_outer):
    normed = norm_rows(stream, gain, bias).astype(BF)
    pre_act = mm(normed, w_inner) + b_inner
    active = jax.nn.gelu(pre_act).astype(BF)
    return mm(active, w_outer) + b_outer, (normed, pre_act, active)


def dense_backward(grad_in, stream, gain, saved, w_inner, w_outer):
    normed, pre_act, active = saved
    outer = grad_in.astype(BF)
    active_grad = mm_t(outer, w_outer)
    inner = jax.vjp(jax.nn.gelu, pre_act)[1](active_grad)[0].astype(BF)
    normed_grad = mm_t(inner, w_inner)
    back, gain_grad, bias_grad = norm_back(stream, gain, normed_grad)
    return (
        grad_in + back,
        (normed, inner),
        (active, outer),
        jnp.sum(inner.astype(F32), 0),
        jnp.sum(outer.astype(F32), 0),
        gain_grad,
        bias_grad,
    )


def over_shards(block):
    r = block.shape[0]
    parts = jnp.moveaxis(block.reshape(r, 4, 256), 1, 0)
    got = lax.all_to_all(parts, SHARD, 0, 0, tiled=True)
    return jnp.sum(got.astype(F32), 0)


def on_device(
    pixels,
    latents,
    input_segments,
    latent_offsets,
    pixel_gain,
    pixel_shift,
    query_weight,
    key_weight,
    value_weight,
    cross_output,
    cross_up,
    cross_down,
    self_projection,
    self_output,
    self_up,
    self_down,
    norm_gains,
    norm_shifts,
    dense_bias,
    cotangent,
):
    width = 1024
    channels = pixels.shape[2]
    head_dim = width // HEADS
    place = lax.axis_index(CTX)

    small = jnp.concatenate(
        [
            query_weight,
            key_weight,
            value_weight,
            norm_gains,
            norm_shifts,
            dense_bias,
            jnp.zeros((1664 - 1024 - 2 * channels - 12, 256), BF),
        ],
        0,
    )
    whole_a = gather_shards(small)
    whole_b = gather_shards(jnp.concatenate([cross_output, cross_up, cross_down], 0))
    proj = gather_shards(self_projection)
    whole_c = gather_shards(jnp.concatenate([self_output, self_up, self_down], 0))
    wq = whole_a[:1024]
    wk = whole_a[1024 : 1024 + channels]
    wv = whole_a[1024 + channels : 1024 + 2 * channels]
    base = 1024 + 2 * channels
    gains = whole_a[base : base + 4].astype(F32)
    shifts = whole_a[base + 4 : base + 8].astype(F32)
    biases = whole_a[base + 8 : base + 12].astype(F32)
    co, cu, cd = whole_b[:1024], whole_b[1024:2048], whole_b[2048:]
    so, su, sd = whole_c[:1024], whole_c[1024:2048], whole_c[2048:]

    both = spread(jnp.concatenate([latents[0], cotangent[0]], 1))
    lat = both[:, :width].astype(F32)
    cot = both[:, width:].astype(F32)
    ids = jnp.sum(
        (latent_offsets[0][None, 1:] <= jnp.arange(512, dtype=jnp.int32)[:, None]).astype(jnp.int32),
        1,
    )

    pixel_in = pixels[0].astype(F32)
    pgain, pshift = pixel_gain.astype(F32), pixel_shift.astype(F32)
    pl_low = norm_rows(pixel_in, pgain, pshift).astype(BF)

    cross_low = norm_rows(lat, gains[0], shifts[0]).astype(BF)
    query = mm(cross_low, wq).astype(BF)
    folded = (mm_t(query, wk) * (width**-0.5)).astype(BF)
    allowed = ids[:, None] == input_segments[0][None, :]
    scores = jnp.where(allowed, mm_t(folded, pl_low), -1e30)
    top = jnp.max(scores, -1, keepdims=True)
    weights = jnp.where(allowed, jnp.exp(scores - top), 0.0)
    total = jnp.sum(weights, -1, keepdims=True)
    some = total > 0
    mixed = mm(weights.astype(BF), pl_low) / jnp.where(some, total, 1.0)
    log_sum = jnp.where(some, top + jnp.log(jnp.where(some, total, 1.0)), -1e30)
    got = lax.all_to_all(
        jnp.concatenate([mixed.astype(BF), *in_three(log_sum)], 1), CTX, 0, 0, tiled=True
    ).astype(F32)
    got = got.reshape(32, 16, channels + 3)
    logs = jnp.sum(got[:, :, channels:], -1, keepdims=True)
    most = jnp.max(logs, 0, keepdims=True)
    share = jnp.exp(logs - most)
    share_sum = jnp.sum(share, 0)
    own_mixed = jnp.sum(share * got[:, :, :channels], 0) / share_sum
    own_log = most[0] + jnp.log(share_sum)
    got = spread(jnp.concatenate([own_mixed.astype(BF), *in_three(own_log)], 1))
    blend = got[:, :channels]
    log_all = jnp.sum(got[:, channels:].astype(F32), -1, keepdims=True)

    attended = mm(blend, wv).astype(BF)
    one = lat + mm(attended, co)
    delta, saved_one = dense_forward(one, gains[1], shifts[1], cu, biases[0], cd, biases[1])
    two = one + delta
    self_low = norm_rows(two, gains[2], shifts[2]).astype(BF)
    triple = mm(self_low, proj).astype(BF)
    sq = triple[:, :width].reshape(512, HEADS, head_dim)
    sk = triple[:, width : 2 * width].reshape(512, HEADS, head_dim)
    sv = triple[:, 2 * width :].reshape(512, HEADS, head_dim)
    same = (ids[:, None] == ids[None, :])[None]
    self_scale = head_dim**-0.5
    raw = jnp.einsum("qhd,khd->hqk", sq, sk, preferred_element_type=F32) * self_scale
    raw = jnp.where(same, raw, -1e30)
    self_top = jnp.max(raw, -1, keepdims=True)
    self_exp = jnp.exp(raw - self_top)
    probs = self_exp / jnp.sum(self_exp, -1, keepdims=True)
    plow = probs.astype(BF)
    att = (
        jnp.einsum("hqk,khd->qhd", plow, sv, preferred_element_type=F32)
        .reshape(512, width)
        .astype(BF)
    )
    three = two + mm(att, so)
    delta, saved_two = dense_forward(three, gains[3], shifts[3], su, biases[2], sd, biases[3])
    result = three + delta

    g3, in2, out2, bi2, bo2, gg3, gs3 = dense_backward(cot, three, gains[3], saved_two, su, sd)
    so_low = g3.astype(BF)
    att_grad = mm_t(so_low, so).astype(BF).reshape(512, HEADS, head_dim)
    prob_grad = jnp.einsum("qhd,khd->hqk", att_grad, sv, preferred_element_type=F32)
    inner = jnp.sum(probs * prob_grad, -1, keepdims=True)
    sgrad = (probs * (prob_grad - inner)).astype(BF)
    dq = jnp.einsum("hqk,khd->qhd", sgrad, sk, preferred_element_type=F32) * self_scale
    dk = jnp.einsum("hqk,qhd->khd", sgrad, sq, preferred_element_type=F32) * self_scale
    dv = jnp.einsum("hqk,qhd->khd", plow, att_grad, preferred_element_type=F32)
    triple_grad = jnp.concatenate(
        [dq.reshape(512, width), dk.reshape(512, width), dv.reshape(512, width)], 1
    ).astype(BF)
    back, gg2, gs2 = norm_back(two, gains[2], mm_t(triple_grad, proj))
    g2 = g3 + back
    g1, in1, out1, bi1, bo1, gg1, gs1 = dense_backward(g2, one, gains[1], saved_one, cu, cd)
    co_low = g1.astype(BF)
    cross_grad = mm_t(co_low, co).astype(BF)
    blend_grad = mm_t(cross_grad, wv).astype(BF)

    inner = jnp.sum(blend_grad.astype(F32) * blend.astype(F32), -1, keepdims=True)
    cprobs = jnp.where(allowed, jnp.exp(scores - log_all), 0.0)
    cgrad = (cprobs * (mm_t(blend_grad, pl_low) - inner)).astype(BF)
    folded_part = mm(cgrad, pl_low) * (width**-0.5)
    pl_grad = t_mm(cgrad, folded) + t_mm(cprobs.astype(BF), blend_grad)
    pixel_stream, pg, ps = norm_back(pixel_in, pgain, pl_grad)
    sums = jnp.stack([*in_three(pg), *in_three(ps)])
    sent = jnp.concatenate(
        [
            folded_part.astype(BF).reshape(32, 16, channels),
            jnp.broadcast_to(sums[None], (32, 6, channels)),
        ],
        1,
    )
    got = jnp.sum(lax.all_to_all(sent, CTX, 0, 0, tiled=True).astype(F32), 0)
    own_folded = got[:16].astype(BF)
    pixel_sums = jnp.stack([got[16] + got[17] + got[18], got[19] + got[20] + got[21]])
    folded_grad = spread(own_folded)
    query_grad = mm(folded_grad, wk).astype(BF)
    back, gg0, gs0 = norm_back(lat, gains[0], mm_t(query_grad, wq))
    latent_total = lax.dynamic_slice_in_dim(g1 + back, place * 16, 16, 0)

    def rows32(pair):
        left, right = pair
        return t_mm(lax.dynamic_slice_in_dim(left, place * 32, 32, 1), right)

    def rows9(left, right):
        padded = jnp.pad(left, ((0, 0), (0, 288 - channels)))
        return t_mm(lax.dynamic_slice_in_dim(padded, place * 9, 9, 1), right)

    tg = rows32((self_low, triple_grad)).reshape(32, 4, 3, 256)
    tg = jnp.moveaxis(tg, 2, 0).reshape(96, 1024)
    early = jnp.concatenate(
        [
            rows32(in2),
            rows32(out2),
            rows32((att, so_low)),
            tg,
            rows32(in1),
            rows32(out1),
            rows32((attended, co_low)),
            rows9(blend, cross_grad),
        ],
        0,
    ).astype(BF)
    early = spread(over_shards(early).astype(BF)).reshape(32, -1, 256)
    ps_parts = jnp.pad(jnp.stack(in_three(pixel_sums)).reshape(6, channels), ((0, 2), (0, 1024 - channels)))
    shards_sum = jnp.concatenate(
        [
            rows32((cross_low, query_grad)),
            rows9(folded_grad, query),
            jnp.stack([gg0, gg1, gg2, gg3]),
            jnp.stack([gs0, gs1, gs2, gs3]),
            jnp.stack([bi1, bo1, bi2, bo2]),
        ],
        0,
    ).astype(BF)
    parts = jnp.moveaxis(shards_sum.reshape(-1, 4, 256), 1, 0)
    pad = jnp.pad(jnp.stack(in_three(pixel_sums)).reshape(6, channels), ((0, 0), (0, 512 - channels)))
    pad = jnp.broadcast_to(pad.reshape(1, 12, 256), (4, 12, 256))
    got = lax.all_to_all(jnp.concatenate([parts, pad], 1), SHARD, 0, 0, tiled=True).astype(F32)
    got = jnp.sum(got, 0)
    late = spread(got[:41].astype(BF)).reshape(32, 41, 256)
    norm_part = got[41:53]
    pix = jnp.sum(got[53:65].reshape(3, 2, 512), 0)[:, :channels]

    def grown(block, first, rows=32):
        return block[:, first : first + rows].reshape(32 * rows, 256).astype(F32)

    proj_grad = jnp.concatenate([grown(early, 96 + 32 * i) for i in range(3)], 1)
    return (
        lax.dynamic_slice_in_dim(result, place * 16, 16, 0).astype(BF)[None],
        latent_total.astype(BF)[None],
        pixel_stream.astype(BF)[None],
        pix[0],
        pix[1],
        grown(late, 0),
        grown(late, 32, 9)[:channels],
        grown(early, 288, 9)[:channels],
        grown(early, 256),
        grown(early, 192),
        grown(early, 224),
        proj_grad,
        grown(early, 64),
        grown(early, 0),
        grown(early, 32),
        norm_part[:4],
        norm_part[4:8],
        norm_part[8:12],
    )


def solution(mesh):
    fine = Mesh(mesh.devices.reshape(4, 2, 4, 2, 2), CTX + SHARD)
    rows = P(SHARD, CTX, None)
    cols = P(None, SHARD)
    return jax.shard_map(
        on_device,
        mesh=fine,
        in_specs=(
            rows,
            rows,
            P(SHARD, CTX),
            P(SHARD, None),
            P(),
            P(),
            *([cols] * 13),
            rows,
        ),
        out_specs=(rows, rows, rows, P(), P(), *([cols] * 13)),
        check_vma=False,
    )
```

```python
import jax
import jax.numpy as jnp
from jax import lax
from jax.experimental import pallas as pl
from jax.experimental.pallas import tpu as pltpu
from jax.sharding import Mesh, PartitionSpec as P

BF = jnp.bfloat16
F32 = jnp.float32
HEADS = 8
CHANNELS = 261
HBM = pl.BlockSpec(memory_space=pl.ANY)
VM = pl.BlockSpec(memory_space=pltpu.VMEM)
SM = pl.BlockSpec(memory_space=pltpu.SMEM)
STEP = 64


def nn(a, b):
    return lax.dot_general(a, b, (((1,), (0,)), ((), ())), preferred_element_type=F32)


def nt(a, b):
    return lax.dot_general(a, b, (((1,), (1,)), ((), ())), preferred_element_type=F32)


def tn(a, b):
    return lax.dot_general(a, b, (((0,), (0,)), ((), ())), preferred_element_type=F32)


def tile(j):
    return pl.ds(pl.multiple_of(j * 256, 256), 256)


def load(dst, where, own, there, pieces, unit, sems, first, width=256, offset=0):
    copies = []

    def go(part, rows, slot):
        at = pl.multiple_of(where[slot] * width + offset, 256)
        copy = pltpu.make_async_copy(part, dst.at[rows, :, pl.ds(at, 256)], sems.at[len(copies)])
        copy.start()
        copies.append(copy)

    cols = pl.ds(offset, 256)
    go(own.at[:, :, cols], pl.ds(0, 8), 1)
    go(there.at[:, :, cols], pl.ds(0, 8), 2)
    for k in range(8):
        go(pieces[k].at[unit], pl.ds(2 * where[first + k % 4], 2), 3 + k // 4)
    return copies


def arrive(copies):
    for copy in copies:
        copy.wait()


def by_cols(x, w, then):
    for j in range(w.shape[2] // 256):
        cols = slice(j * 256, j * 256 + 256)
        then(cols, nn(x[...], w[:, :, cols].reshape(1024, 256)))


def by_rows(dy, w, then):
    for j in range(4):
        block = w[2 * j : 2 * j + 2].reshape(256, w.shape[2])
        then(slice(j * 256, j * 256 + 256), nt(dy[...], block))


def norm_stats(v):
    center = jnp.mean(v, -1, keepdims=True)
    centred = v - center
    scale = lax.rsqrt(jnp.mean(centred * centred, -1, keepdims=True) + 1e-05)
    return centred * scale, scale


def norm_into(out, stream, gain, bias):
    @pl.loop(0, 512 // STEP, unroll=4)
    def _(i):
        rows = pl.ds(pl.multiple_of(i * STEP, STEP), STEP)
        hat, _ = norm_stats(stream[rows, :].astype(F32))
        out[rows, :] = (hat * gain + bias).astype(BF)


def norm_grad(out, low, stream, gain, grad, carry):
    def body(i, sums):
        rows = pl.ds(pl.multiple_of(i * STEP, STEP), STEP)
        hat, scale = norm_stats(stream[rows, :])
        dy = grad[rows, :]
        dhat = dy * gain
        back = scale * (
            dhat
            - jnp.mean(dhat, -1, keepdims=True)
            - hat * jnp.mean(dhat * hat, -1, keepdims=True)
        )
        new = carry[rows, :].astype(F32) + back
        out[rows, :] = new
        low[rows, :] = new.astype(BF)
        fold = lambda v: jnp.sum(v.reshape(STEP // 8, 8, 1024), 0)
        return sums[0] + fold(dy * hat), sums[1] + fold(dy)

    zero = jnp.zeros((8, 1024), F32)
    a, b = lax.fori_loop(0, 512 // STEP, body, (zero, zero), unroll=4)
    return jnp.sum(a, 0, keepdims=True), jnp.sum(b, 0, keepdims=True)


ROOT = 0.7978845608028654


def gelu(u):
    return 0.5 * u * (1.0 + jnp.tanh(ROOT * (u + 0.044715 * (u * u * u))))


def gelu_slope(u):
    t = jnp.tanh(ROOT * (u + 0.044715 * (u * u * u)))
    return 0.5 * (1.0 + t) + 0.5 * u * (1.0 - t * t) * (ROOT * (1.0 + 0.134145 * (u * u)))


def pick(x, where, slot=15, count=64):
    lane = lax.broadcasted_iota(jnp.int32, (count, x.shape[1]), 1)
    row = lax.broadcasted_iota(jnp.int32, (count, x.shape[1]), 0)
    chosen = jnp.where(lane == row + where[slot] * count, 1.0, 0.0).astype(BF)
    return nt(chosen, x[...]).astype(BF)


def call(body, outs, scratch, args, specs, flops):
    return pl.pallas_call(
        body,
        out_shape=outs,
        in_specs=specs,
        out_specs=[VM] * len(outs),
        scratch_shapes=scratch,
        compiler_params=pltpu.CompilerParams(vmem_limit_bytes=58 * 1024 * 1024),
        cost_estimate=pl.CostEstimate(flops=flops, bytes_accessed=20_000_000, transcendentals=0),
    )(*args)


def s(shape, dtype):
    return jax.ShapeDtypeStruct(shape, dtype)


def head_probs(q, k, idk, idr, raw, probs, low):
    raw[...] = nt(k, q)
    for j in range(4):
        cols = slice(j * 128, j * 128 + 128)
        v = jnp.where(idk[...] == idr[:, cols], raw[:, cols] * (128**-0.5), -1e30)
        e = jnp.exp(v - jnp.max(v, 0, keepdims=True))
        p = e * (1.0 / jnp.sum(e, 0, keepdims=True))
        if probs is not None:
            probs[:, cols] = p
        low[:, cols] = p.astype(BF)


def lanes(h, base=0):
    return pl.ds(pl.multiple_of(base + h * 128, 128), 128)


def as_row(column):
    return jnp.broadcast_to(column, (512, 128)).T[0:1, :]


def layers(where, blend, rows, vecs, idk, idr, pixels, pl_low, folded, gain, segb, fours, groups, pieces):
    def body(where, blend, both, vecs, idk, idr, pixels, pl_low, folded, gain, segb, *refs):
        fours, refs = refs[:4], refs[4:]
        first, proj, second, refs = refs[:6], refs[6:8], refs[8:14], refs[14:]
        first_pieces, proj_pieces, second_pieces, refs = refs[:8], refs[8:16], refs[16:24], refs[24:]
        result, g1_own, grads_two, grads_proj, grads_one, small, pixel_grad, part, psum = refs[:9]
        w0, w1, w2, wp, one, pre, two, three, pre_two, dn, g, cross, low, act, att, att_grad, inner = refs[9:26]
        triple, dt, raw, probs, plow, slow, t_att, t_norm, t_act, t_low, t_self, sems = refs[26:]
        lat, cot = both.at[:, 0:1024], both.at[:, 1024:2048]
        own = pl.ds(pl.multiple_of(where[0] * 16, 16), 16)
        mix = blend[:, 0:CHANNELS]

        def fetch(dst, group, pieces, i, slot):
            return load(dst, where, group[i], group[i + 3], pieces, i, sems.at[slot], 5)

        c0, c1, c2 = (fetch(w, first, first_pieces, i, i) for i, w in enumerate((w0, w1, w2)))
        cp = []
        for j in range(3):
            cp += load(wp, where, proj[0], proj[1], proj_pieces, j, sems.at[3 + j], 9, 768, 256 * j)

        for i in range(4):
            cross[:, tile(where[1 + i])] = nn(mix, fours[i][288 : 288 + CHANNELS, :]).astype(BF)
        arrive(c0)

        def put(cols, acc):
            one[:, cols] = lat[:, cols].astype(F32) + acc

        by_cols(cross, w0, put)
        c0 = fetch(w0, second, second_pieces, 0, 6)
        t_att[...] = pick(cross, where)
        norm_into(low, one, vecs[1:2, :], vecs[5:6, :])
        arrive(c1)

        def put(cols, acc):
            u = acc + vecs[8:9, cols]
            pre[:, cols] = u
            act[:, cols] = gelu(u).astype(BF)

        by_cols(low, w1, put)
        c1 = fetch(w1, second, second_pieces, 1, 7)
        t_norm[...] = pick(low, where)
        arrive(c2)

        def put(cols, acc):
            two[:, cols] = one[:, cols] + (acc + vecs[9:10, cols])

        by_cols(act, w2, put)
        c2 = fetch(w2, second, second_pieces, 2, 8)
        t_act[...] = pick(act, where)

        norm_into(low, two, vecs[2:3, :], vecs[6:7, :])
        t_low[...] = pick(low, where)
        arrive(cp)

        def put(cols, acc):
            triple[:, cols] = acc.astype(BF)

        by_cols(low, wp, put)

        @pl.loop(0, HEADS // 2)
        def _(i):
            for p in range(2):
                h = 2 * i + p
                head_probs(triple[:, lanes(h)], triple[:, lanes(h, 1024)], idk, idr, raw.at[p], None, plow.at[p])
                att[:, lanes(h)] = tn(triple[:, lanes(h, 2048)], plow[p]).T.astype(BF)

        t_self[...] = pick(att, where)

        arrive(c0)

        def put(cols, acc):
            three[:, cols] = two[:, cols] + acc

        by_cols(att, w0, put)
        norm_into(low, three, vecs[3:4, :], vecs[7:8, :])
        arrive(c1)

        def put(cols, acc):
            u = acc + vecs[10:11, cols]
            pre_two[:, cols] = u
            act[:, cols] = gelu(u).astype(BF)

        by_cols(low, w1, put)
        arrive(c2)

        @pl.loop(0, 4)
        def _(j):
            acc = nn(act[own, :], w2[:, :, tile(j)].reshape(1024, 256)) + vecs[11:12, tile(j)]
            result[:, tile(j)] = (three[own, tile(j)] + acc).astype(BF)

        small[3:4, :] = jnp.sum(cot[...].astype(F32), 0, keepdims=True)
        grads_two[64:128, :] = nn(pick(act, where), cot[...]).astype(BF)

        def put(cols, acc):
            du = (acc * gelu_slope(pre_two[:, cols])).astype(BF)
            inner[:, cols] = du
            small[2:3, cols] = jnp.sum(du.astype(F32), 0, keepdims=True)

        by_rows(cot, w2, put)
        c2 = fetch(w2, first, first_pieces, 2, 9)
        grads_two[0:64, :] = nn(pick(low, where), inner[...]).astype(BF)

        def put(cols, acc):
            dn[:, cols] = acc

        by_rows(inner, w1, put)
        c1 = fetch(w1, first, first_pieces, 1, 10)
        da, db = norm_grad(g, low, three, vecs[3:4, :], dn, cot)
        small[0:1, :] = da
        small[1:2, :] = db
        grads_two[128:192, :] = nn(t_self[...], low[...]).astype(BF)

        def put(cols, acc):
            att_grad[:, cols] = acc.astype(BF)

        by_rows(low, w0, put)
        c0 = fetch(w0, first, first_pieces, 0, 11)

        scale = 128**-0.5

        @pl.loop(0, HEADS // 2)
        def _(i):
            for p in range(2):
                h = 2 * i + p
                q, k, v = (triple[:, lanes(h, b)] for b in (0, 1024, 2048))
                da = att_grad[:, lanes(h)]
                head_probs(q, k, idk, idr, raw.at[p], probs.at[p], plow.at[p])
                raw[p] = nt(v, da)
                for j in range(4):
                    cols = slice(j * 128, j * 128 + 128)
                    pr, dp = probs[p, :, cols], raw[p, :, cols]
                    slow[p, :, cols] = (pr * (dp - jnp.sum(pr * dp, 0, keepdims=True))).astype(BF)
                dt[:, lanes(h)] = (tn(k, slow[p]).T * scale).astype(BF)
                dt[:, lanes(h, 1024)] = (nn(slow[p], q) * scale).astype(BF)
                dt[:, lanes(h, 2048)] = nn(plow[p], da).astype(BF)

        for j in range(12):
            cols = slice(j * 256, j * 256 + 256)
            grads_proj[:, cols] = nn(t_low[...], dt[:, cols]).astype(BF)

        def put(cols, acc):
            dn[:, cols] = acc

        by_rows(dt, wp, put)
        da, db = norm_grad(g, low, two, vecs[2:3, :], dn, g)
        small[8:9, :] = da
        small[9:10, :] = db

        small[19:20, :] = jnp.sum(low[...].astype(F32), 0, keepdims=True)
        grads_one[64:128, :] = nn(t_act[...], low[...]).astype(BF)
        arrive(c2)

        def put(cols, acc):
            du = (acc * gelu_slope(pre[:, cols])).astype(BF)
            inner[:, cols] = du
            small[18:19, cols] = jnp.sum(du.astype(F32), 0, keepdims=True)

        by_rows(low, w2, put)
        grads_one[0:64, :] = nn(t_norm[...], inner[...]).astype(BF)
        arrive(c1)

        def put(cols, acc):
            dn[:, cols] = acc

        by_rows(inner, w1, put)
        da, db = norm_grad(g, low, one, vecs[1:2, :], dn, g)
        small[16:17, :] = da
        small[17:18, :] = db
        g1_own[...] = g[own, :]
        grads_one[128:192, :] = nn(t_att[...], low[...]).astype(BF)
        arrive(c0)

        def put(cols, acc):
            cross[:, cols] = acc.astype(BF)

        by_rows(low, w0, put)
        grads_one[192:224, :] = nn(pick(mix, where, 15, 32), cross[...]).astype(BF)
        total = nt(cross[:, tile(where[1])], fours[0][288 : 288 + CHANNELS, :])
        for i in range(1, 4):
            total += nt(cross[:, tile(where[1 + i])], fours[i][288 : 288 + CHANNELS, :])
        mix_grad = total.astype(BF)

        delta = as_row(jnp.sum(mix_grad.astype(F32) * mix.astype(F32), -1, keepdims=True))
        logs = as_row(jnp.sum(blend[:, CHANNELS : CHANNELS + 3].astype(F32), -1, keepdims=True))
        raw[0] = nt(pl_low[...], folded[...])
        raw[1] = nt(pl_low[...], mix_grad)
        for j in range(4):
            cols = slice(j * 128, j * 128 + 128)
            p = jnp.where(segb[...] == idr[:, cols], jnp.exp(raw[0, :, cols] - logs[:, cols]), 0.0)
            plow[0, :, cols] = p.astype(BF)
            slow[0, :, cols] = (p * (raw[1, :, cols] - delta[:, cols])).astype(BF)
        part[...] = (tn(pl_low[...], slow[0]).T * (1024**-0.5)).astype(BF)
        dn[:, 0:CHANNELS] = nn(slow[0], folded[...]) + nn(plow[0], mix_grad)

        def body(i, sums):
            rows = pl.ds(pl.multiple_of(i * STEP, STEP), STEP)
            hat, scale = norm_stats(pixels[rows, :].astype(F32))
            dy = dn[rows, 0:CHANNELS]
            dhat = dy * gain[...]
            back = scale * (
                dhat
                - jnp.mean(dhat, -1, keepdims=True)
                - hat * jnp.mean(dhat * hat, -1, keepdims=True)
            )
            pixel_grad[rows, :] = back.astype(BF)
            return sums[0] + jnp.sum(dy * hat, 0, keepdims=True), sums[1] + jnp.sum(dy, 0, keepdims=True)

        zero = jnp.zeros((1, CHANNELS), F32)
        a, b = lax.fori_loop(0, 512 // STEP, body, (zero, zero), unroll=4)
        psum[0:1, :] = a
        psum[1:2, :] = b

    return call(
        body,
        [
            s((16, 1024), BF),
            s((16, 1024), F32),
            s((192, 1024), BF),
            s((64, 3072), BF),
            s((224, 1024), BF),
            s((24, 1024), F32),
            s((512, CHANNELS), BF),
            s((512, CHANNELS), BF),
            s((2, CHANNELS), F32),
        ],
        [pltpu.VMEM((8, 128, 1024), BF)] * 3
        + [pltpu.VMEM((8, 128, 3072), BF)]
        + [pltpu.VMEM((512, 1024), F32)] * 7
        + [pltpu.VMEM((512, 1024), BF)] * 6
        + [pltpu.VMEM((512, 3072), BF)] * 2
        + [pltpu.VMEM((2, 512, 512), F32)] * 2
        + [pltpu.VMEM((2, 512, 512), BF)] * 2
        + [pltpu.VMEM((64, 512), BF)] * 5
        + [pltpu.SemaphoreType.DMA((12, 10))],
        (where, blend, rows, vecs, idk, idr, pixels, pl_low, folded, gain, segb, *fours, *groups, *pieces),
        [SM] + [VM] * 14 + [HBM] * 38,
        30_000_000_000,
    )


def front(where, lat, pixels, gain, bias, segb, idr, query_four, small_four):
    def body(where, rows, pixels, gain, bias, segb, idr, *refs):
        lat = rows.at[:, 0:1024]
        wq, fours, refs = refs[:4], refs[4:8], refs[8:]
        vecs, query, folded, pl_low, sent, tcross, low, raw, pt, turned = refs
        for k in range(4):
            vecs[:, tile(where[1 + k])] = fours[k][0:16, :].astype(F32)[0:12, :]
        norm_into(low, lat, vecs[0:1, :], vecs[4:5, :])

        @pl.loop(0, 512 // STEP, unroll=4)
        def _(i):
            rows = pl.ds(pl.multiple_of(i * STEP, STEP), STEP)
            hat, _ = norm_stats(pixels[rows, :].astype(F32))
            pl_low[rows, :] = (hat * gain[...] + bias[...]).astype(BF)

        total = None
        for k in range(4):
            cols = slice(k * 256, k * 256 + 256)
            query[:, cols] = nn(low[...], wq[k][...]).astype(BF)
            term = nt(query[:, cols], fours[k][16 : 16 + CHANNELS, :])
            total = term if total is None else total + term
        folded[...] = (total * (1024**-0.5)).astype(BF)
        raw[...] = nt(pl_low[...], folded[...])
        for j in range(4):
            cols = slice(j * 128, j * 128 + 128)
            allowed = segb[...] == idr[:, cols]
            v = jnp.where(allowed, raw[:, cols], -1e30)
            top = jnp.max(v, 0, keepdims=True)
            e = jnp.where(allowed, jnp.exp(v - top), 0.0)
            pt[:, cols] = e.astype(BF)
            weight = jnp.sum(e, 0, keepdims=True)
            some = weight > 0.0
            safe = jnp.where(some, weight, 1.0)
            logs = jnp.where(some, top + jnp.log(safe), -1e30)
            turned[0:CHANNELS, cols] = tn(pl_low[...], pt[:, cols]) * (1.0 / safe)
            high = logs.astype(BF).astype(F32)
            middle = (logs - high).astype(BF).astype(F32)
            turned[CHANNELS : CHANNELS + 1, cols] = high
            turned[CHANNELS + 1 : CHANNELS + 2, cols] = middle
            turned[CHANNELS + 2 : CHANNELS + 3, cols] = logs - high - middle
        sent[...] = turned[...].T.astype(BF)
        tcross[...] = pick(low, where, 0, 32)

    return call(
        body,
        [
            s((12, 1024), F32),
            s((512, 1024), BF),
            s((512, CHANNELS), BF),
            s((512, CHANNELS), BF),
            s((512, CHANNELS + 3), BF),
            s((32, 512), BF),
        ],
        [
            pltpu.VMEM((512, 1024), BF),
            pltpu.VMEM((512, 512), F32),
            pltpu.VMEM((512, 512), BF),
            pltpu.VMEM((CHANNELS + 3, 512), F32),
        ],
        (where, lat, pixels, gain, bias, segb, idr, *query_four, *small_four),
        [SM] + [VM] * 14,
        2_000_000_000,
    )


def finish(where, folded_grad, lat, vecs, tcross, query, g1_own, query_four, small_four):
    def body(where, folded_grad, rows, vecs, tcross, query, g1_own, *refs):
        lat = rows.at[:, 0:1024]
        wq, fours, refs = refs[:4], refs[4:8], refs[8:]
        latent, late, small, grad, dn = refs
        fg = folded_grad[...]
        for k in range(4):
            cols = slice(k * 256, k * 256 + 256)
            grad[:, cols] = nn(fg, fours[k][16 : 16 + CHANNELS, :]).astype(BF)
        for j in range(4):
            cols = slice(j * 256, j * 256 + 256)
            total = nt(grad[:, 0:256], wq[0][cols, :])
            for k in range(1, 4):
                total += nt(grad[:, k * 256 : k * 256 + 256], wq[k][cols, :])
            dn[:, cols] = total
        late[0:32, :] = nn(tcross[...], grad[...]).astype(BF)
        late[32:48, :] = nn(pick(fg, where, 0, 16), query[...]).astype(BF)

        def body(i, sums):
            rows = pl.ds(pl.multiple_of(i * STEP, STEP), STEP)
            hat, _ = norm_stats(lat[rows, :].astype(F32))
            dy = dn[rows, :]
            fold = lambda v: jnp.sum(v.reshape(STEP // 8, 8, 1024), 0)
            return sums[0] + fold(dy * hat), sums[1] + fold(dy)

        zero = jnp.zeros((8, 1024), F32)
        a, b = lax.fori_loop(0, 512 // STEP, body, (zero, zero), unroll=4)
        small[0:1, :] = jnp.sum(a, 0, keepdims=True)
        small[1:2, :] = jnp.sum(b, 0, keepdims=True)
        own = pl.ds(pl.multiple_of(where[0] * 16, 16), 16)
        hat, scale = norm_stats(lat[own, :].astype(F32))
        dhat = dn[own, :] * vecs[0:1, :]
        back = scale * (
            dhat
            - jnp.mean(dhat, -1, keepdims=True)
            - hat * jnp.mean(dhat * hat, -1, keepdims=True)
        )
        latent[...] = (g1_own[...] + back).astype(BF)

    return call(
        body,
        [s((16, 1024), BF), s((48, 1024), BF), s((2, 1024), F32)],
        [pltpu.VMEM((512, 1024), BF), pltpu.VMEM((512, 1024), F32)],
        (where, folded_grad, lat, vecs, tcross, query, g1_own, *query_four, *small_four),
        [SM] + [VM] * 14,
        2_500_000_000,
    )


def collect(where, cross, projection, later):
    def body(where, *refs):
        cross, projection, later, outs, sems = refs[:3], refs[3], refs[4:7], refs[7:10], refs[10]
        units = [(w, 0) for w in cross], [(projection, 256 * j) for j in range(3)], [(w, 0) for w in later]
        copies = []
        for g in range(3):
            quarter = where[9] if g == 1 else where[5]
            row = pl.multiple_of(quarter * 256, 256)
            for u, (w, col) in enumerate(units[g]):
                part = w.at[pl.ds(row, 256), pl.ds(col, 256)]
                copies.append(pltpu.make_async_copy(part, outs[g].at[u], sems.at[g, u]))
        for copy in copies:
            copy.start()
        arrive(copies)

    return pl.pallas_call(
        body,
        out_shape=[s((3, 256, 256), BF)] * 3,
        in_specs=[SM] + [HBM] * 7,
        out_specs=[VM] * 3,
        scratch_shapes=[pltpu.SemaphoreType.DMA((3, 3))],
        compiler_params=pltpu.CompilerParams(vmem_limit_bytes=58 * 1024 * 1024),
        cost_estimate=pl.CostEstimate(flops=0, bytes_accessed=2_400_000, transcendentals=0),
    )(where, *cross, projection, *later)


def settle(where, blocks, groups, shapes, places):
    def body(where, *refs):
        blocks, refs = refs[: len(refs) - 2 * len(shapes) - 1], refs[len(refs) - 2 * len(shapes) - 1 :]
        n = len(shapes)
        outs, bufs, sems = refs[:n], refs[n : 2 * n], refs[2 * n]
        copies = []
        last = [o for units in groups for o, _, _ in units]
        for units, where_from in zip(groups, places):
            base = 0
            for o, col, rows in units:
                short = shapes[o][0] == CHANNELS
                for which, index, place in where_from:
                    at = place(where)
                    if isinstance(at, int):
                        if short and at * rows >= CHANNELS:
                            continue
                        at = at * rows
                    else:
                        at = jnp.minimum(at, CHANNELS // rows + 1) if short else at
                        at = pl.multiple_of(at * rows, rows)
                    part = blocks[which][(*index, slice(base, base + rows))]
                    bufs[o][pl.ds(at, rows), col : col + 256] = part.astype(F32)
                base += rows
                last.pop(0)
                if short:
                    outs[o][...] = bufs[o][0:CHANNELS, :]
                elif o not in last:
                    copy = pltpu.make_async_copy(bufs[o], outs[o], sems.at[o])
                    copy.start()
                    copies.append(copy)
        arrive(copies)

    return pl.pallas_call(
        body,
        out_shape=[s(shape, F32) for shape in shapes],
        in_specs=[SM] + [VM] * len(blocks),
        out_specs=[VM if shape[0] == CHANNELS else HBM for shape in shapes],
        scratch_shapes=[pltpu.VMEM((320 if r == CHANNELS else r, c), F32) for r, c in shapes]
        + [pltpu.SemaphoreType.DMA((len(shapes),))],
        compiler_params=pltpu.CompilerParams(vmem_limit_bytes=58 * 1024 * 1024),
        cost_estimate=pl.CostEstimate(flops=0, bytes_accessed=10_000_000, transcendentals=0),
    )(where, *blocks)


CTX = ("x", "zl", "y")
SHARD = ("zh", "core")


def shift(value, axis, by):
    count = lax.axis_size(axis)
    return lax.ppermute(value, axis, [(i, (i + by) % count) for i in range(count)])


def facing(value):
    return lax.ppermute(value, ("zl", "zh"), [(i, 3 - i) for i in range(4)])


def spread(rows):
    return lax.all_to_all(jnp.tile(rows, (32, 1)), CTX, 0, 0, tiled=True)


def in_three(value):
    high = lax.reduce_precision(value, 8, 7)
    rest = value - high
    middle = lax.reduce_precision(rest, 8, 7)
    return high.astype(BF), middle.astype(BF), (rest - middle).astype(BF)


def with_core(parts):
    return lax.ppermute(jnp.stack([parts[1], parts[3]]), SHARD, [(i, i ^ 1) for i in range(4)])


def with_facing(parts, got):
    near, far = parts[0].astype(F32) + got[0].astype(F32), parts[2].astype(F32) + got[1].astype(F32)
    return near, lax.ppermute(far.astype(BF), SHARD, [(i, i ^ 2) for i in range(4)])


def ring(rows, axis):
    return [rows] + [shift(rows, axis, k) for k in (1, 2, 3)]


def paired(rows, axis):
    two = jnp.stack([rows, lax.ppermute(rows, axis, [(i, i ^ 1) for i in range(4)])])
    return jnp.concatenate([two, lax.ppermute(two, axis, [(i, i ^ 3) for i in range(4)])])


def after(values, *events):
    return lax.optimization_barrier((values, events))[0]


def true_parts(block, own, width=256):
    rows = block.shape[0]
    return [lax.dynamic_slice(block, (0, (own ^ k) * width), (rows, width)) for k in range(4)]


def on_device(
    pixels,
    latents,
    input_segments,
    latent_offsets,
    pixel_gain,
    pixel_shift,
    query_weight,
    key_weight,
    value_weight,
    cross_output,
    cross_up,
    cross_down,
    self_projection,
    self_output,
    self_up,
    self_down,
    norm_gains,
    norm_shifts,
    dense_bias,
    cotangent,
):
    width = 1024
    channels = pixels.shape[2]
    ix, iy = lax.axis_index("x"), lax.axis_index("y")
    place = lax.axis_index(CTX)
    own = lax.axis_index(SHARD)
    where = jnp.stack(
        [place]
        + [own ^ k for k in range(4)]
        + [(ix + 4 - k) % 4 for k in range(4)]
        + [(iy + 4 - k) % 4 for k in range(4)]
        + [place * 0] * 2
        + [ix * 4 + iy]
    ).astype(jnp.int32)

    small_own = jnp.concatenate(
        [
            norm_gains,
            norm_shifts,
            dense_bias,
            jnp.pad(key_weight, ((4, 272 - channels), (0, 0))),
            jnp.pad(value_weight, ((0, 272 - channels), (0, 0))),
        ],
        0,
    )
    both_rows = spread(jnp.concatenate([latents[0], cotangent[0]], 1))
    small_other, query_other = after((facing(small_own), facing(query_weight)), both_rows)
    small_four = [small_own, shift(small_own, "core", 1), small_other, shift(small_other, "core", 1)]
    query_four = [query_weight, shift(query_weight, "core", 1), query_other, shift(query_other, "core", 1)]

    where_now = after(where, small_own)
    send_one, send_proj, send_two = collect(
        where_now,
        [cross_output, cross_up, cross_down],
        self_projection,
        [self_output, self_up, self_down],
    )
    face_one, face_proj, face_two = facing(send_one), facing(send_proj), facing(send_two)

    def both(*weights):
        there = [shift(w, "core", 1) for w in weights]
        return [w.reshape(8, 128, -1) for w in (*weights, *there)]

    group_one = both(cross_output, cross_up, cross_down)
    group_proj = both(self_projection)
    group_two = both(self_output, self_up, self_down)

    ids = jnp.sum(
        (latent_offsets[0][None, 1:] <= jnp.arange(512, dtype=jnp.int32)[:, None]).astype(jnp.int32),
        1,
    )
    idk = jnp.broadcast_to(ids[:, None], (512, 128))
    idr = ids[None, :]

    segb = jnp.broadcast_to(input_segments[0][:, None], (512, 128))
    pgain, pbias = pixel_gain.astype(F32)[None], pixel_shift.astype(F32)[None]

    vecs, query, folded, pl_low, sent, tcross = front(
        where, after(both_rows, face_one), pixels[0], pgain, pbias, segb, idr, query_four, small_four
    )
    got = lax.all_to_all(sent, CTX, 0, 0, tiled=True)
    pieces_one = ring(face_one, "x")
    got = after(got, pieces_one)
    got = got.astype(F32)
    got = got.reshape(32, 16, channels + 3)
    logs = jnp.sum(got[:, :, channels:], -1, keepdims=True)
    most = jnp.max(logs, 0, keepdims=True)
    share = jnp.exp(logs - most)
    share_sum = jnp.sum(share, 0)
    own_mixed = jnp.sum(share * got[:, :, :channels], 0) / share_sum
    own_log = most[0] + jnp.log(share_sum)
    packed = jnp.concatenate([own_mixed.astype(BF), *in_three(own_log)], 1)
    pieces_proj, pieces_two = ring(after(face_proj, sent), "y"), ring(after(face_two, sent), "x")
    blend = spread(after(packed, pieces_proj))

    there_one, there_proj, there_two = (
        [shift(piece, "core", 1) for piece in pieces]
        for pieces in after((pieces_one, pieces_proj, pieces_two), own_log)
    )

    def halved(pieces, there):
        return [piece.reshape(3, 2, 128, 256) for piece in (*pieces, *there)]

    result, g1_own, grads_two, grads_proj, grads_one, small_grads, pixel_grad, part, psum = layers(
        where, blend, both_rows, vecs, idk, idr, pixels[0], pl_low, folded, pgain, segb, small_four,
        (*group_one, *group_proj, *group_two),
        (*halved(pieces_one, there_one), *halved(pieces_proj, there_proj), *halved(pieces_two, there_two)),
    )
    small_two, small_proj, small_one = small_grads[:8], small_grads[8:16], small_grads[16:]

    parts = []
    for k in range(4):
        third = lax.dynamic_slice(grads_proj, (0, (own ^ k) * 768), (64, 768))
        thirds = [third[:, 256 * j : 256 * j + 256] for j in range(3)]
        at = (0, (own ^ k) * 256)
        parts.append(
            jnp.concatenate(
                [lax.dynamic_slice(grads_two, at, (192, 256)), *thirds, lax.dynamic_slice(grads_one, at, (224, 256))], 0
            )
        )
    got_core = with_core(parts)

    sums = jnp.stack(in_three(psum)).reshape(6, channels)
    sent = jnp.concatenate(
        [
            part.reshape(32, 16, channels),
            jnp.broadcast_to(sums[None], (32, 6, channels)),
        ],
        1,
    )
    got = jnp.sum(lax.all_to_all(sent, CTX, 0, 0, tiled=True).astype(F32), 0)
    pixel_sums = (got[16:18] + got[18:20]) + got[20:22]
    near, far = with_facing(parts, got_core)
    total = (near + far.astype(F32)).astype(BF)
    first, second = paired(total[:320], "x"), paired(total[320:], "y")
    own_folded = after(got[:16].astype(BF), first, second)
    folded_grad = spread(own_folded)
    first = ring(after(first, folded_grad), "y")
    second = ring(after(second, folded_grad), "x")
    latent_total, late, small_zero = finish(
        where, folded_grad, both_rows, vecs, tcross, query, g1_own, query_four, small_four
    )
    small = jnp.stack(
        [
            *(small_zero[0], small_one[0], small_proj[0], small_two[0]),
            *(small_zero[1], small_one[1], small_proj[1], small_two[1]),
            *(small_one[2], small_one[3], small_two[2], small_two[3]),
        ]
    ).astype(BF)

    def sixfold(value):
        parts = jnp.pad(jnp.concatenate(in_three(value), 0), ((0, 0), (0, 512 - channels)))
        return parts.reshape(12, 256)

    def whole(parts):
        return jnp.sum(parts.reshape(3, 2, 512).astype(F32), 0)[:, :channels]

    small_parts = true_parts(small, own)
    parts = [
        jnp.concatenate([late[:, 256 * k : 256 * k + 256], small_parts[k]], 0) for k in range(4)
    ]
    got = lax.ppermute(
        jnp.concatenate([parts[1], parts[3], sixfold(pixel_sums)], 0), SHARD, [(i, i ^ 1) for i in range(4)]
    )
    near = parts[0].astype(F32) + got[:60].astype(F32)
    far = parts[2].astype(F32) + got[60:120].astype(F32)
    pixel_sums = pixel_sums + whole(got[120:])
    got = lax.ppermute(
        jnp.concatenate([far.astype(BF), sixfold(pixel_sums)], 0), SHARD, [(i, i ^ 2) for i in range(4)]
    )
    late_sum = near + got[:60].astype(F32)
    norm_part = late_sum[48:60]
    pix = pixel_sums + whole(got[60:])

    last = spread(late_sum[:48].astype(BF)).reshape(32, 48, 256)
    tall, few = (1024, 256), (channels, 256)
    bits = (0, 1, 3, 2)
    su, sd, so, proj, cu, cd, co, v = settle(
        where,
        [*first, *second],
        [
            [(0, 0, 64), (1, 0, 64), (2, 0, 64), (3, 0, 64), (3, 256, 64)],
            [(3, 512, 64), (4, 0, 64), (5, 0, 64), (6, 0, 64), (7, 0, 32)],
        ],
        [tall, tall, tall, (1024, 768), tall, tall, tall, few],
        [
            [(k, (b,), lambda where, k=k, b=b: (where[5] ^ bits[b]) * 4 + where[9 + k]) for k in range(4) for b in range(4)],
            [(4 + k, (b,), lambda where, k=k, b=b: where[5 + k] * 4 + (where[9] ^ bits[b])) for k in range(4) for b in range(4)],
        ],
    )
    q, k = settle(
        where,
        [last],
        [[(0, 0, 32), (1, 0, 16)]],
        [tall, few],
        [[(0, (c,), lambda where, at=c: at) for c in range(32)]],
    )
    return (
        result[None],
        latent_total[None],
        pixel_grad[None],
        pix[0],
        pix[1],
        q,
        k,
        v,
        co,
        cu,
        cd,
        proj,
        so,
        su,
        sd,
        norm_part[:4],
        norm_part[4:8],
        norm_part[8:12],
    )


def solution(mesh):
    fine = Mesh(mesh.devices.reshape(4, 2, 4, 2, 2), CTX + SHARD)
    rows = P(SHARD, CTX, None)
    cols = P(None, SHARD)
    return jax.shard_map(
        on_device,
        mesh=fine,
        in_specs=(
            rows,
            rows,
            P(SHARD, CTX),
            P(SHARD, None),
            P(),
            P(),
            *([cols] * 13),
            rows,
        ),
        out_specs=(rows, rows, rows, P(), P(), *([cols] * 13)),
        check_vma=False,
    )
```

```python
import jax
import jax.numpy as jnp
from jax import lax
from jax.experimental import pallas as pl
from jax.experimental.pallas import tpu as pltpu
from jax.sharding import Mesh, PartitionSpec as P

BF = jnp.bfloat16
F32 = jnp.float32
HEADS = 8
CHANNELS = 261
HBM = pl.BlockSpec(memory_space=pl.ANY)
VM = pl.BlockSpec(memory_space=pltpu.VMEM)
SM = pl.BlockSpec(memory_space=pltpu.SMEM)
STEP = 64


def nn(a, b):
    return lax.dot_general(a, b, (((1,), (0,)), ((), ())), preferred_element_type=F32)


def nt(a, b):
    return lax.dot_general(a, b, (((1,), (1,)), ((), ())), preferred_element_type=F32)


def tn(a, b):
    return lax.dot_general(a, b, (((0,), (0,)), ((), ())), preferred_element_type=F32)


def tile(j):
    return pl.ds(pl.multiple_of(j * 256, 256), 256)


def load(dst, where, own, there, pieces, unit, sems, width=256, offset=0):
    copies = []

    def go(part, rows, slot):
        at = pl.multiple_of(where[slot] * width + offset, 256)
        copy = pltpu.make_async_copy(part, dst.at[rows, :, pl.ds(at, 256)], sems.at[len(copies)])
        copy.start()
        copies.append(copy)

    cols = pl.ds(offset, 256)
    go(own.at[:, :, cols], pl.ds(0, 8), 1)
    go(there.at[:, :, cols], pl.ds(0, 8), 2)
    for k in range(4):
        go(pieces[k].at[unit], pl.ds(4 * where[13 + k % 2], 4), 3 + k // 2)
    return copies


def arrive(copies):
    for copy in copies:
        copy.wait()


def by_cols(x, w, then):
    for j in range(w.shape[2] // 256):
        cols = slice(j * 256, j * 256 + 256)
        then(cols, nn(x[...], w[:, :, cols].reshape(1024, 256)))


def by_rows(dy, w, then):
    for j in range(4):
        block = w[2 * j : 2 * j + 2].reshape(256, w.shape[2])
        then(slice(j * 256, j * 256 + 256), nt(dy[...], block))


def norm_stats(v):
    center = jnp.mean(v, -1, keepdims=True)
    centred = v - center
    scale = lax.rsqrt(jnp.mean(centred * centred, -1, keepdims=True) + 1e-05)
    return centred * scale, scale


def norm_into(out, stream, gain, bias):
    @pl.loop(0, 512 // STEP, unroll=4)
    def _(i):
        rows = pl.ds(pl.multiple_of(i * STEP, STEP), STEP)
        hat, _ = norm_stats(stream[rows, :].astype(F32))
        out[rows, :] = (hat * gain + bias).astype(BF)


def norm_grad(out, low, stream, gain, grad, carry):
    def body(i, sums):
        rows = pl.ds(pl.multiple_of(i * STEP, STEP), STEP)
        hat, scale = norm_stats(stream[rows, :])
        dy = grad[rows, :]
        dhat = dy * gain
        back = scale * (
            dhat
            - jnp.mean(dhat, -1, keepdims=True)
            - hat * jnp.mean(dhat * hat, -1, keepdims=True)
        )
        new = carry[rows, :].astype(F32) + back
        out[rows, :] = new
        low[rows, :] = new.astype(BF)
        fold = lambda v: jnp.sum(v.reshape(STEP // 8, 8, 1024), 0)
        return sums[0] + fold(dy * hat), sums[1] + fold(dy)

    zero = jnp.zeros((8, 1024), F32)
    a, b = lax.fori_loop(0, 512 // STEP, body, (zero, zero), unroll=4)
    return jnp.sum(a, 0, keepdims=True), jnp.sum(b, 0, keepdims=True)


ROOT = 0.7978845608028654


def gelu(u):
    return 0.5 * u * (1.0 + jnp.tanh(ROOT * (u + 0.044715 * (u * u * u))))


def gelu_slope(u):
    t = jnp.tanh(ROOT * (u + 0.044715 * (u * u * u)))
    return 0.5 * (1.0 + t) + 0.5 * u * (1.0 - t * t) * (ROOT * (1.0 + 0.134145 * (u * u)))


def pick(x, where, slot=15, count=64):
    lane = lax.broadcasted_iota(jnp.int32, (count, x.shape[1]), 1)
    row = lax.broadcasted_iota(jnp.int32, (count, x.shape[1]), 0)
    chosen = jnp.where(lane == row + where[slot] * count, 1.0, 0.0).astype(BF)
    return nt(chosen, x[...]).astype(BF)


def call(body, outs, scratch, args, specs, flops):
    return pl.pallas_call(
        body,
        out_shape=outs,
        in_specs=specs,
        out_specs=[VM] * len(outs),
        scratch_shapes=scratch,
        compiler_params=pltpu.CompilerParams(vmem_limit_bytes=58 * 1024 * 1024),
        cost_estimate=pl.CostEstimate(flops=flops, bytes_accessed=20_000_000, transcendentals=0),
    )(*args)


def s(shape, dtype):
    return jax.ShapeDtypeStruct(shape, dtype)


def head_probs(q, k, idk, idr, raw, probs, low):
    raw[...] = nt(k, q)
    for j in range(4):
        cols = slice(j * 128, j * 128 + 128)
        v = jnp.where(idk[...] == idr[:, cols], raw[:, cols] * (128**-0.5), -1e30)
        e = jnp.exp(v - jnp.max(v, 0, keepdims=True))
        p = e * (1.0 / jnp.sum(e, 0, keepdims=True))
        if probs is not None:
            probs[:, cols] = p
        low[:, cols] = p.astype(BF)


def lanes(h, base=0):
    return pl.ds(pl.multiple_of(base + h * 128, 128), 128)


def as_row(column):
    return jnp.broadcast_to(column, (512, 128)).T[0:1, :]


def layers(where, blend, rows, vecs, idk, idr, pixels, pl_low, folded, gain, segb, fours, groups, pieces):
    def body(where, blend, both, vecs, idk, idr, pixels, pl_low, folded, gain, segb, *refs):
        fours, refs = refs[:4], refs[4:]
        first, proj, second, refs = refs[:6], refs[6:8], refs[8:14], refs[14:]
        first_pieces, proj_pieces, second_pieces, refs = refs[:4], refs[4:8], refs[8:12], refs[12:]
        result, g1_own, grads_two, grads_proj, grads_one, small, pixel_grad, part, psum = refs[:9]
        w0, w1, w2, wp, one, pre, two, three, pre_two, dn, g, cross, low, act, att, att_grad, inner = refs[9:26]
        triple, dt, raw, probs, plow, slow, t_att, t_norm, t_act, t_low, t_self, sems = refs[26:]
        lat, cot = both.at[:, 0:1024], both.at[:, 1024:2048]
        own = pl.ds(pl.multiple_of(where[0] * 16, 16), 16)
        mix = blend[:, 0:CHANNELS]

        def fetch(dst, group, pieces, i, slot):
            return load(dst, where, group[i], group[i + 3], pieces, i, sems.at[slot])

        c0, c1, c2 = (fetch(w, first, first_pieces, i, i) for i, w in enumerate((w0, w1, w2)))
        cp = []
        for j in range(3):
            cp += load(wp, where, proj[0], proj[1], proj_pieces, j, sems.at[3 + j], 768, 256 * j)

        for i in range(4):
            cross[:, tile(where[1 + i])] = nn(mix, fours[i][288 : 288 + CHANNELS, :]).astype(BF)
        arrive(c0)

        def put(cols, acc):
            one[:, cols] = lat[:, cols].astype(F32) + acc

        by_cols(cross, w0, put)
        c0 = fetch(w0, second, second_pieces, 0, 6)
        t_att[...] = pick(cross, where)
        norm_into(low, one, vecs[1:2, :], vecs[5:6, :])
        arrive(c1)

        def put(cols, acc):
            u = acc + vecs[8:9, cols]
            pre[:, cols] = u
            act[:, cols] = gelu(u).astype(BF)

        by_cols(low, w1, put)
        c1 = fetch(w1, second, second_pieces, 1, 7)
        t_norm[...] = pick(low, where)
        arrive(c2)

        def put(cols, acc):
            two[:, cols] = one[:, cols] + (acc + vecs[9:10, cols])

        by_cols(act, w2, put)
        c2 = fetch(w2, second, second_pieces, 2, 8)
        t_act[...] = pick(act, where)

        norm_into(low, two, vecs[2:3, :], vecs[6:7, :])
        t_low[...] = pick(low, where)
        arrive(cp)

        def put(cols, acc):
            triple[:, cols] = acc.astype(BF)

        by_cols(low, wp, put)

        @pl.loop(0, HEADS // 2)
        def _(i):
            for p in range(2):
                h = 2 * i + p
                head_probs(triple[:, lanes(h)], triple[:, lanes(h, 1024)], idk, idr, raw.at[p], None, plow.at[p])
                att[:, lanes(h)] = tn(triple[:, lanes(h, 2048)], plow[p]).T.astype(BF)

        t_self[...] = pick(att, where)

        arrive(c0)

        def put(cols, acc):
            three[:, cols] = two[:, cols] + acc

        by_cols(att, w0, put)
        norm_into(low, three, vecs[3:4, :], vecs[7:8, :])
        arrive(c1)

        def put(cols, acc):
            u = acc + vecs[10:11, cols]
            pre_two[:, cols] = u
            act[:, cols] = gelu(u).astype(BF)

        by_cols(low, w1, put)
        arrive(c2)

        @pl.loop(0, 4)
        def _(j):
            acc = nn(act[own, :], w2[:, :, tile(j)].reshape(1024, 256)) + vecs[11:12, tile(j)]
            result[:, tile(j)] = (three[own, tile(j)] + acc).astype(BF)

        small[3:4, :] = jnp.sum(cot[...].astype(F32), 0, keepdims=True)
        grads_two[64:128, :] = nn(pick(act, where), cot[...]).astype(BF)

        def put(cols, acc):
            du = (acc * gelu_slope(pre_two[:, cols])).astype(BF)
            inner[:, cols] = du
            small[2:3, cols] = jnp.sum(du.astype(F32), 0, keepdims=True)

        by_rows(cot, w2, put)
        c2 = fetch(w2, first, first_pieces, 2, 9)
        grads_two[0:64, :] = nn(pick(low, where), inner[...]).astype(BF)

        def put(cols, acc):
            dn[:, cols] = acc

        by_rows(inner, w1, put)
        c1 = fetch(w1, first, first_pieces, 1, 10)
        da, db = norm_grad(g, low, three, vecs[3:4, :], dn, cot)
        small[0:1, :] = da
        small[1:2, :] = db
        grads_two[128:192, :] = nn(t_self[...], low[...]).astype(BF)

        def put(cols, acc):
            att_grad[:, cols] = acc.astype(BF)

        by_rows(low, w0, put)
        c0 = fetch(w0, first, first_pieces, 0, 11)

        scale = 128**-0.5

        @pl.loop(0, HEADS // 2)
        def _(i):
            for p in range(2):
                h = 2 * i + p
                q, k, v = (triple[:, lanes(h, b)] for b in (0, 1024, 2048))
                da = att_grad[:, lanes(h)]
                head_probs(q, k, idk, idr, raw.at[p], probs.at[p], plow.at[p])
                raw[p] = nt(v, da)
                for j in range(4):
                    cols = slice(j * 128, j * 128 + 128)
                    pr, dp = probs[p, :, cols], raw[p, :, cols]
                    slow[p, :, cols] = (pr * (dp - jnp.sum(pr * dp, 0, keepdims=True))).astype(BF)
                dt[:, lanes(h)] = (tn(k, slow[p]).T * scale).astype(BF)
                dt[:, lanes(h, 1024)] = (nn(slow[p], q) * scale).astype(BF)
                dt[:, lanes(h, 2048)] = nn(plow[p], da).astype(BF)

        for j in range(12):
            cols = slice(j * 256, j * 256 + 256)
            grads_proj[:, cols] = nn(t_low[...], dt[:, cols]).astype(BF)

        def put(cols, acc):
            dn[:, cols] = acc

        by_rows(dt, wp, put)
        da, db = norm_grad(g, low, two, vecs[2:3, :], dn, g)
        small[8:9, :] = da
        small[9:10, :] = db

        small[19:20, :] = jnp.sum(low[...].astype(F32), 0, keepdims=True)
        grads_one[64:128, :] = nn(t_act[...], low[...]).astype(BF)
        arrive(c2)

        def put(cols, acc):
            du = (acc * gelu_slope(pre[:, cols])).astype(BF)
            inner[:, cols] = du
            small[18:19, cols] = jnp.sum(du.astype(F32), 0, keepdims=True)

        by_rows(low, w2, put)
        grads_one[0:64, :] = nn(t_norm[...], inner[...]).astype(BF)
        arrive(c1)

        def put(cols, acc):
            dn[:, cols] = acc

        by_rows(inner, w1, put)
        da, db = norm_grad(g, low, one, vecs[1:2, :], dn, g)
        small[16:17, :] = da
        small[17:18, :] = db
        g1_own[...] = g[own, :]
        grads_one[128:192, :] = nn(t_att[...], low[...]).astype(BF)
        arrive(c0)

        def put(cols, acc):
            cross[:, cols] = acc.astype(BF)

        by_rows(low, w0, put)
        grads_one[192:224, :] = nn(pick(mix, where, 15, 32), cross[...]).astype(BF)
        total = nt(cross[:, tile(where[1])], fours[0][288 : 288 + CHANNELS, :])
        for i in range(1, 4):
            total += nt(cross[:, tile(where[1 + i])], fours[i][288 : 288 + CHANNELS, :])
        mix_grad = total.astype(BF)

        delta = as_row(jnp.sum(mix_grad.astype(F32) * mix.astype(F32), -1, keepdims=True))
        logs = as_row(jnp.sum(blend[:, CHANNELS : CHANNELS + 3].astype(F32), -1, keepdims=True))
        raw[0] = nt(pl_low[...], folded[...])
        raw[1] = nt(pl_low[...], mix_grad)
        for j in range(4):
            cols = slice(j * 128, j * 128 + 128)
            p = jnp.where(segb[...] == idr[:, cols], jnp.exp(raw[0, :, cols] - logs[:, cols]), 0.0)
            plow[0, :, cols] = p.astype(BF)
            slow[0, :, cols] = (p * (raw[1, :, cols] - delta[:, cols])).astype(BF)
        part[...] = (tn(pl_low[...], slow[0]).T * (1024**-0.5)).astype(BF)
        dn[:, 0:CHANNELS] = nn(slow[0], folded[...]) + nn(plow[0], mix_grad)

        def body(i, sums):
            rows = pl.ds(pl.multiple_of(i * STEP, STEP), STEP)
            hat, scale = norm_stats(pixels[rows, :].astype(F32))
            dy = dn[rows, 0:CHANNELS]
            dhat = dy * gain[...]
            back = scale * (
                dhat
                - jnp.mean(dhat, -1, keepdims=True)
                - hat * jnp.mean(dhat * hat, -1, keepdims=True)
            )
            pixel_grad[rows, :] = back.astype(BF)
            return sums[0] + jnp.sum(dy * hat, 0, keepdims=True), sums[1] + jnp.sum(dy, 0, keepdims=True)

        zero = jnp.zeros((1, CHANNELS), F32)
        a, b = lax.fori_loop(0, 512 // STEP, body, (zero, zero), unroll=4)
        psum[0:1, :] = a
        psum[1:2, :] = b

    return call(
        body,
        [
            s((16, 1024), BF),
            s((16, 1024), F32),
            s((192, 1024), BF),
            s((64, 3072), BF),
            s((224, 1024), BF),
            s((24, 1024), F32),
            s((512, CHANNELS), BF),
            s((512, CHANNELS), BF),
            s((2, CHANNELS), F32),
        ],
        [pltpu.VMEM((8, 128, 1024), BF)] * 3
        + [pltpu.VMEM((8, 128, 3072), BF)]
        + [pltpu.VMEM((512, 1024), F32)] * 7
        + [pltpu.VMEM((512, 1024), BF)] * 6
        + [pltpu.VMEM((512, 3072), BF)] * 2
        + [pltpu.VMEM((2, 512, 512), F32)] * 2
        + [pltpu.VMEM((2, 512, 512), BF)] * 2
        + [pltpu.VMEM((64, 512), BF)] * 5
        + [pltpu.SemaphoreType.DMA((12, 6))],
        (where, blend, rows, vecs, idk, idr, pixels, pl_low, folded, gain, segb, *fours, *groups, *pieces),
        [SM] + [VM] * 14 + [HBM] * 26,
        30_000_000_000,
    )


def front(where, lat, pixels, gain, bias, segb, idr, query_four, small_four):
    def body(where, rows, pixels, gain, bias, segb, idr, *refs):
        lat = rows.at[:, 0:1024]
        wq, fours, refs = refs[:4], refs[4:8], refs[8:]
        vecs, query, folded, pl_low, sent, tcross, low, raw, pt, turned = refs
        for k in range(4):
            vecs[:, tile(where[1 + k])] = fours[k][0:16, :].astype(F32)[0:12, :]
        norm_into(low, lat, vecs[0:1, :], vecs[4:5, :])

        @pl.loop(0, 512 // STEP, unroll=4)
        def _(i):
            rows = pl.ds(pl.multiple_of(i * STEP, STEP), STEP)
            hat, _ = norm_stats(pixels[rows, :].astype(F32))
            pl_low[rows, :] = (hat * gain[...] + bias[...]).astype(BF)

        total = None
        for k in range(4):
            cols = slice(k * 256, k * 256 + 256)
            query[:, cols] = nn(low[...], wq[k][...]).astype(BF)
            term = nt(query[:, cols], fours[k][16 : 16 + CHANNELS, :])
            total = term if total is None else total + term
        folded[...] = (total * (1024**-0.5)).astype(BF)
        raw[...] = nt(pl_low[...], folded[...])
        for j in range(4):
            cols = slice(j * 128, j * 128 + 128)
            allowed = segb[...] == idr[:, cols]
            v = jnp.where(allowed, raw[:, cols], -1e30)
            top = jnp.max(v, 0, keepdims=True)
            e = jnp.where(allowed, jnp.exp(v - top), 0.0)
            pt[:, cols] = e.astype(BF)
            weight = jnp.sum(e, 0, keepdims=True)
            some = weight > 0.0
            safe = jnp.where(some, weight, 1.0)
            logs = jnp.where(some, top + jnp.log(safe), -1e30)
            turned[0:CHANNELS, cols] = tn(pl_low[...], pt[:, cols]) * (1.0 / safe)
            high = logs.astype(BF).astype(F32)
            middle = (logs - high).astype(BF).astype(F32)
            turned[CHANNELS : CHANNELS + 1, cols] = high
            turned[CHANNELS + 1 : CHANNELS + 2, cols] = middle
            turned[CHANNELS + 2 : CHANNELS + 3, cols] = logs - high - middle
        sent[...] = turned[...].T.astype(BF)
        tcross[...] = pick(low, where, 0, 32)

    return call(
        body,
        [
            s((12, 1024), F32),
            s((512, 1024), BF),
            s((512, CHANNELS), BF),
            s((512, CHANNELS), BF),
            s((512, CHANNELS + 3), BF),
            s((32, 512), BF),
        ],
        [
            pltpu.VMEM((512, 1024), BF),
            pltpu.VMEM((512, 512), F32),
            pltpu.VMEM((512, 512), BF),
            pltpu.VMEM((CHANNELS + 3, 512), F32),
        ],
        (where, lat, pixels, gain, bias, segb, idr, *query_four, *small_four),
        [SM] + [VM] * 14,
        20_000_000_000,
    )


def finish(where, folded_grad, lat, vecs, tcross, query, g1_own, query_four, small_four):
    def body(where, folded_grad, rows, vecs, tcross, query, g1_own, *refs):
        lat = rows.at[:, 0:1024]
        wq, fours, refs = refs[:4], refs[4:8], refs[8:]
        latent, late, small, grad, dn = refs
        fg = folded_grad[...]
        for k in range(4):
            cols = slice(k * 256, k * 256 + 256)
            grad[:, cols] = nn(fg, fours[k][16 : 16 + CHANNELS, :]).astype(BF)
        for j in range(4):
            cols = slice(j * 256, j * 256 + 256)
            total = nt(grad[:, 0:256], wq[0][cols, :])
            for k in range(1, 4):
                total += nt(grad[:, k * 256 : k * 256 + 256], wq[k][cols, :])
            dn[:, cols] = total
        late[0:32, :] = nn(tcross[...], grad[...]).astype(BF)
        late[32:48, :] = nn(pick(fg, where, 0, 16), query[...]).astype(BF)

        def body(i, sums):
            rows = pl.ds(pl.multiple_of(i * STEP, STEP), STEP)
            hat, _ = norm_stats(lat[rows, :].astype(F32))
            dy = dn[rows, :]
            fold = lambda v: jnp.sum(v.reshape(STEP // 8, 8, 1024), 0)
            return sums[0] + fold(dy * hat), sums[1] + fold(dy)

        zero = jnp.zeros((8, 1024), F32)
        a, b = lax.fori_loop(0, 512 // STEP, body, (zero, zero), unroll=4)
        small[0:1, :] = jnp.sum(a, 0, keepdims=True)
        small[1:2, :] = jnp.sum(b, 0, keepdims=True)
        own = pl.ds(pl.multiple_of(where[0] * 16, 16), 16)
        hat, scale = norm_stats(lat[own, :].astype(F32))
        dhat = dn[own, :] * vecs[0:1, :]
        back = scale * (
            dhat
            - jnp.mean(dhat, -1, keepdims=True)
            - hat * jnp.mean(dhat * hat, -1, keepdims=True)
        )
        latent[...] = (g1_own[...] + back).astype(BF)

    return call(
        body,
        [s((16, 1024), BF), s((48, 1024), BF), s((2, 1024), F32)],
        [pltpu.VMEM((512, 1024), BF), pltpu.VMEM((512, 1024), F32)],
        (where, folded_grad, lat, vecs, tcross, query, g1_own, *query_four, *small_four),
        [SM] + [VM] * 14,
        2_500_000_000,
    )


def collect(where, cross, projection, later):
    def body(where, *refs):
        cross, projection, later, outs, sems = refs[:3], refs[3], refs[4:7], refs[7:10], refs[10]
        units = [(w, 0) for w in cross], [(projection, 256 * j) for j in range(3)], [(w, 0) for w in later]
        row = pl.multiple_of(where[14] * 512, 512)
        copies = []
        for g in range(3):
            for u, (w, col) in enumerate(units[g]):
                part = w.at[pl.ds(row, 512), pl.ds(col, 256)]
                copies.append(pltpu.make_async_copy(part, outs[g].at[u], sems.at[g, u]))
        for copy in copies:
            copy.start()
        arrive(copies)

    return pl.pallas_call(
        body,
        out_shape=[s((3, 512, 256), BF)] * 3,
        in_specs=[SM] + [HBM] * 7,
        out_specs=[VM] * 3,
        scratch_shapes=[pltpu.SemaphoreType.DMA((3, 3))],
        compiler_params=pltpu.CompilerParams(vmem_limit_bytes=58 * 1024 * 1024),
        cost_estimate=pl.CostEstimate(flops=0, bytes_accessed=4_800_000, transcendentals=0),
    )(where, *cross, projection, *later)


def settle(where, blocks, groups, shapes, places):
    def body(where, *refs):
        blocks, refs = refs[: len(refs) - 2 * len(shapes) - 1], refs[len(refs) - 2 * len(shapes) - 1 :]
        n = len(shapes)
        outs, bufs, sems = refs[:n], refs[n : 2 * n], refs[2 * n]
        copies = []
        last = [o for units in groups for o, _, _ in units]
        for units, where_from in zip(groups, places):
            base = 0
            for o, col, rows in units:
                short = shapes[o][0] == CHANNELS
                for which, index, place in where_from:
                    at = place(where)
                    if isinstance(at, int):
                        if short and at * rows >= CHANNELS:
                            continue
                        at = at * rows
                    else:
                        at = jnp.minimum(at, CHANNELS // rows + 1) if short else at
                        at = pl.multiple_of(at * rows, rows)
                    part = blocks[which][(*index, slice(base, base + rows))]
                    bufs[o][pl.ds(at, rows), col : col + 256] = part.astype(F32)
                base += rows
                last.pop(0)
                if short:
                    outs[o][...] = bufs[o][0:CHANNELS, :]
                elif o not in last:
                    copy = pltpu.make_async_copy(bufs[o], outs[o], sems.at[o])
                    copy.start()
                    copies.append(copy)
        arrive(copies)

    return pl.pallas_call(
        body,
        out_shape=[s(shape, F32) for shape in shapes],
        in_specs=[SM] + [VM] * len(blocks),
        out_specs=[VM if shape[0] == CHANNELS else HBM for shape in shapes],
        scratch_shapes=[pltpu.VMEM((320 if r == CHANNELS else r, c), F32) for r, c in shapes]
        + [pltpu.SemaphoreType.DMA((len(shapes),))],
        compiler_params=pltpu.CompilerParams(vmem_limit_bytes=58 * 1024 * 1024),
        cost_estimate=pl.CostEstimate(flops=0, bytes_accessed=10_000_000, transcendentals=0),
    )(where, *blocks)


def handed(x):
    def body(x, out):
        out[...] = x[...]

    return pl.pallas_call(
        body,
        out_shape=s(x.shape, x.dtype),
        in_specs=[VM],
        out_specs=VM,
        compiler_params=pltpu.CompilerParams(vmem_limit_bytes=58 * 1024 * 1024),
        cost_estimate=pl.CostEstimate(flops=20_000_000_000, bytes_accessed=1_000_000, transcendentals=0),
    )(x)


CTX = ("x", "zl", "y")
SHARD = ("zh", "core")


def shift(value, axis, by):
    count = lax.axis_size(axis)
    return lax.ppermute(value, axis, [(i, (i + by) % count) for i in range(count)])


def facing(value):
    return lax.ppermute(value, ("zl", "zh"), [(i, 3 - i) for i in range(4)])


def spread(rows):
    return lax.all_to_all(jnp.tile(rows, (32, 1)), CTX, 0, 0, tiled=True)


def in_three(value):
    high = lax.reduce_precision(value, 8, 7)
    rest = value - high
    middle = lax.reduce_precision(rest, 8, 7)
    return high.astype(BF), middle.astype(BF), (rest - middle).astype(BF)


def with_core(parts):
    return lax.ppermute(jnp.stack([parts[1], parts[3]]), SHARD, [(i, i ^ 1) for i in range(4)])


def with_facing(parts, got):
    near, far = parts[0].astype(F32) + got[0].astype(F32), parts[2].astype(F32) + got[1].astype(F32)
    return near, lax.ppermute(far.astype(BF), SHARD, [(i, i ^ 2) for i in range(4)])


def ring(rows, axis):
    return [rows] + [shift(rows, axis, k) for k in (1, 2, 3)]


def paired(rows, axis):
    two = jnp.stack([rows, lax.ppermute(rows, axis, [(i, i ^ 1) for i in range(4)])])
    return jnp.concatenate([two, lax.ppermute(two, axis, [(i, i ^ 3) for i in range(4)])])


def after(values, *events):
    return lax.optimization_barrier((values, events))[0]


def true_parts(block, own, width=256):
    rows = block.shape[0]
    return [lax.dynamic_slice(block, (0, (own ^ k) * width), (rows, width)) for k in range(4)]


def on_device(
    pixels,
    latents,
    input_segments,
    latent_offsets,
    pixel_gain,
    pixel_shift,
    query_weight,
    key_weight,
    value_weight,
    cross_output,
    cross_up,
    cross_down,
    self_projection,
    self_output,
    self_up,
    self_down,
    norm_gains,
    norm_shifts,
    dense_bias,
    cotangent,
):
    width = 1024
    channels = pixels.shape[2]
    ix, iy = lax.axis_index("x"), lax.axis_index("y")
    place = lax.axis_index(CTX)
    own = lax.axis_index(SHARD)
    where = jnp.stack(
        [place]
        + [own ^ k for k in range(4)]
        + [(ix + 4 - k) % 4 for k in range(4)]
        + [(iy + 4 - k) % 4 for k in range(4)]
        + [1 - lax.axis_index("zl"), lax.axis_index("zl")]
        + [ix * 4 + iy]
    ).astype(jnp.int32)

    small_own = jnp.concatenate(
        [
            norm_gains,
            norm_shifts,
            dense_bias,
            jnp.pad(key_weight, ((4, 272 - channels), (0, 0))),
            jnp.pad(value_weight, ((0, 272 - channels), (0, 0))),
        ],
        0,
    )
    both_rows = spread(jnp.concatenate([latents[0], cotangent[0]], 1))
    small_other, query_other = after((facing(small_own), facing(query_weight)), both_rows)
    small_four = [small_own, shift(small_own, "core", 1), small_other, shift(small_other, "core", 1)]
    query_four = [query_weight, shift(query_weight, "core", 1), query_other, shift(query_other, "core", 1)]

    where_now = after(where, small_own)
    send_one, send_proj, send_two = collect(
        where_now,
        [cross_output, cross_up, cross_down],
        self_projection,
        [self_output, self_up, self_down],
    )
    face_one = facing(send_one)

    def both(*weights):
        there = [shift(w, "core", 1) for w in weights]
        return [w.reshape(8, 128, -1) for w in (*weights, *there)]

    group_one = both(cross_output, cross_up, cross_down)
    group_proj = both(self_projection)
    group_two = both(self_output, self_up, self_down)

    ids = jnp.sum(
        (latent_offsets[0][None, 1:] <= jnp.arange(512, dtype=jnp.int32)[:, None]).astype(jnp.int32),
        1,
    )
    idk = jnp.broadcast_to(ids[:, None], (512, 128))
    idr = ids[None, :]

    segb = jnp.broadcast_to(input_segments[0][:, None], (512, 128))
    pgain, pbias = pixel_gain.astype(F32)[None], pixel_shift.astype(F32)[None]

    vecs, query, folded, pl_low, sent, tcross = front(
        where, after(both_rows, face_one), pixels[0], pgain, pbias, segb, idr, query_four, small_four
    )
    face_proj, face_two = facing(send_proj), facing(send_two)
    got = lax.all_to_all(sent, CTX, 0, 0, tiled=True)
    near_one = shift(after(face_one, sent), "zl", 1)
    near_proj = shift(after(face_proj, sent), "zl", 1)
    got = handed(after(got, near_one))
    got = got.astype(F32)
    got = got.reshape(32, 16, channels + 3)
    logs = jnp.sum(got[:, :, channels:], -1, keepdims=True)
    most = jnp.max(logs, 0, keepdims=True)
    share = jnp.exp(logs - most)
    share_sum = jnp.sum(share, 0)
    own_mixed = jnp.sum(share * got[:, :, :channels], 0) / share_sum
    own_log = most[0] + jnp.log(share_sum)
    packed = jnp.concatenate([own_mixed.astype(BF), *in_three(own_log)], 1)
    near_two = shift(after(face_two, got), "zl", 1)
    blend = handed(after(spread(packed), near_proj))

    def halves(face, near):
        pieces = [face, near, shift(face, "core", 1), shift(near, "core", 1)]
        return [piece.reshape(3, 4, 128, 256) for piece in pieces]

    result, g1_own, grads_two, grads_proj, grads_one, small_grads, pixel_grad, part, psum = layers(
        where, blend, both_rows, vecs, idk, idr, pixels[0], pl_low, folded, pgain, segb, small_four,
        (*group_one, *group_proj, *group_two),
        (*halves(face_one, near_one), *halves(face_proj, near_proj), *halves(face_two, near_two)),
    )
    small_two, small_proj, small_one = small_grads[:8], small_grads[8:16], small_grads[16:]

    parts = []
    for k in range(4):
        third = lax.dynamic_slice(grads_proj, (0, (own ^ k) * 768), (64, 768))
        thirds = [third[:, 256 * j : 256 * j + 256] for j in range(3)]
        at = (0, (own ^ k) * 256)
        parts.append(
            jnp.concatenate(
                [lax.dynamic_slice(grads_two, at, (192, 256)), *thirds, lax.dynamic_slice(grads_one, at, (224, 256))], 0
            )
        )
    got_core = with_core(parts)

    sums = jnp.stack(in_three(psum)).reshape(6, channels)
    sent = jnp.concatenate(
        [
            part.reshape(32, 16, channels),
            jnp.broadcast_to(sums[None], (32, 6, channels)),
        ],
        1,
    )
    got = jnp.sum(lax.all_to_all(sent, CTX, 0, 0, tiled=True).astype(F32), 0)
    pixel_sums = (got[16:18] + got[18:20]) + got[20:22]
    near, far = with_facing(parts, got_core)
    total = (near + far.astype(F32)).astype(BF)
    first, second = paired(total[:320], "x"), paired(total[320:], "y")
    own_folded = after(got[:16].astype(BF), first, second)
    folded_grad = spread(own_folded)
    first = ring(after(first, folded_grad), "y")
    second = ring(after(second, folded_grad), "x")
    latent_total, late, small_zero = finish(
        where, folded_grad, both_rows, vecs, tcross, query, g1_own, query_four, small_four
    )
    small = jnp.stack(
        [
            *(small_zero[0], small_one[0], small_proj[0], small_two[0]),
            *(small_zero[1], small_one[1], small_proj[1], small_two[1]),
            *(small_one[2], small_one[3], small_two[2], small_two[3]),
        ]
    ).astype(BF)

    def sixfold(value):
        parts = jnp.pad(jnp.concatenate(in_three(value), 0), ((0, 0), (0, 512 - channels)))
        return parts.reshape(12, 256)

    def whole(parts):
        return jnp.sum(parts.reshape(3, 2, 512).astype(F32), 0)[:, :channels]

    small_parts = true_parts(small, own)
    parts = [
        jnp.concatenate([late[:, 256 * k : 256 * k + 256], small_parts[k]], 0) for k in range(4)
    ]
    got = lax.ppermute(
        jnp.concatenate([parts[1], parts[3], sixfold(pixel_sums)], 0), SHARD, [(i, i ^ 1) for i in range(4)]
    )
    near = parts[0].astype(F32) + got[:60].astype(F32)
    far = parts[2].astype(F32) + got[60:120].astype(F32)
    pixel_sums = pixel_sums + whole(got[120:])
    got = lax.ppermute(
        jnp.concatenate([far.astype(BF), sixfold(pixel_sums)], 0), SHARD, [(i, i ^ 2) for i in range(4)]
    )
    late_sum = near + got[:60].astype(F32)
    norm_part = late_sum[48:60]
    pix = pixel_sums + whole(got[60:])

    last = spread(late_sum[:48].astype(BF)).reshape(32, 48, 256)
    tall, few = (1024, 256), (channels, 256)
    bits = (0, 1, 3, 2)
    su, sd, so, proj, cu, cd, co, v = settle(
        where,
        [*first, *second],
        [
            [(0, 0, 64), (1, 0, 64), (2, 0, 64), (3, 0, 64), (3, 256, 64)],
            [(3, 512, 64), (4, 0, 64), (5, 0, 64), (6, 0, 64), (7, 0, 32)],
        ],
        [tall, tall, tall, (1024, 768), tall, tall, tall, few],
        [
            [(k, (b,), lambda where, k=k, b=b: (where[5] ^ bits[b]) * 4 + where[9 + k]) for k in range(4) for b in range(4)],
            [(4 + k, (b,), lambda where, k=k, b=b: where[5 + k] * 4 + (where[9] ^ bits[b])) for k in range(4) for b in range(4)],
        ],
    )
    q, k = settle(
        where,
        [last],
        [[(0, 0, 32), (1, 0, 16)]],
        [tall, few],
        [[(0, (c,), lambda where, at=c: at) for c in range(32)]],
    )
    return (
        result[None],
        latent_total[None],
        pixel_grad[None],
        pix[0],
        pix[1],
        q,
        k,
        v,
        co,
        cu,
        cd,
        proj,
        so,
        su,
        sd,
        norm_part[:4],
        norm_part[4:8],
        norm_part[8:12],
    )


def solution(mesh):
    fine = Mesh(mesh.devices.reshape(4, 2, 4, 2, 2), CTX + SHARD)
    rows = P(SHARD, CTX, None)
    cols = P(None, SHARD)
    return jax.shard_map(
        on_device,
        mesh=fine,
        in_specs=(
            rows,
            rows,
            P(SHARD, CTX),
            P(SHARD, None),
            P(),
            P(),
            *([cols] * 13),
            rows,
        ),
        out_specs=(rows, rows, rows, P(), P(), *([cols] * 13)),
        check_vma=False,
    )
```

```python
import jax
import jax.numpy as jnp
from jax import lax
from jax.experimental import pallas as pl
from jax.experimental.pallas import tpu as pltpu
from jax.sharding import Mesh, PartitionSpec as P

BF = jnp.bfloat16
F32 = jnp.float32
HEADS = 8
CHANNELS = 261
HBM = pl.BlockSpec(memory_space=pl.ANY)
VM = pl.BlockSpec(memory_space=pltpu.VMEM)
SM = pl.BlockSpec(memory_space=pltpu.SMEM)
STEP = 64


def nn(a, b):
    return lax.dot_general(a, b, (((1,), (0,)), ((), ())), preferred_element_type=F32)


def nt(a, b):
    return lax.dot_general(a, b, (((1,), (1,)), ((), ())), preferred_element_type=F32)


def tn(a, b):
    return lax.dot_general(a, b, (((0,), (0,)), ((), ())), preferred_element_type=F32)


def tile(j):
    return pl.ds(pl.multiple_of(j * 256, 256), 256)


def load(dst, where, own, there, pieces, unit, sems, width=256, offset=0):
    copies = []

    def go(part, rows, slot):
        at = pl.multiple_of(where[slot] * width + offset, 256)
        copy = pltpu.make_async_copy(part, dst.at[rows, :, pl.ds(at, 256)], sems.at[len(copies)])
        copy.start()
        copies.append(copy)

    cols = pl.ds(offset, 256)
    go(own.at[:, :, cols], pl.ds(0, 8), 1)
    go(there.at[:, :, cols], pl.ds(0, 8), 2)
    for k in range(4):
        go(pieces[k].at[unit], pl.ds(4 * where[13 + k % 2], 4), 3 + k // 2)
    return copies


def arrive(copies):
    for copy in copies:
        copy.wait()


def by_cols(x, w, then):
    for j in range(w.shape[2] // 256):
        cols = slice(j * 256, j * 256 + 256)
        then(cols, nn(x[...], w[:, :, cols].reshape(1024, 256)))


def by_rows(dy, w, then):
    for j in range(4):
        block = w[2 * j : 2 * j + 2].reshape(256, w.shape[2])
        then(slice(j * 256, j * 256 + 256), nt(dy[...], block))


def norm_stats(v):
    center = jnp.mean(v, -1, keepdims=True)
    centred = v - center
    scale = lax.rsqrt(jnp.mean(centred * centred, -1, keepdims=True) + 1e-05)
    return centred * scale, scale


def norm_into(out, stream, gain, bias):
    @pl.loop(0, 512 // STEP, unroll=4)
    def _(i):
        rows = pl.ds(pl.multiple_of(i * STEP, STEP), STEP)
        hat, _ = norm_stats(stream[rows, :].astype(F32))
        out[rows, :] = (hat * gain + bias).astype(BF)


def norm_grad(out, low, stream, gain, grad, carry):
    def body(i, sums):
        rows = pl.ds(pl.multiple_of(i * STEP, STEP), STEP)
        hat, scale = norm_stats(stream[rows, :])
        dy = grad[rows, :]
        dhat = dy * gain
        back = scale * (
            dhat
            - jnp.mean(dhat, -1, keepdims=True)
            - hat * jnp.mean(dhat * hat, -1, keepdims=True)
        )
        new = carry[rows, :].astype(F32) + back
        out[rows, :] = new
        low[rows, :] = new.astype(BF)
        fold = lambda v: jnp.sum(v.reshape(STEP // 8, 8, 1024), 0)
        return sums[0] + fold(dy * hat), sums[1] + fold(dy)

    zero = jnp.zeros((8, 1024), F32)
    a, b = lax.fori_loop(0, 512 // STEP, body, (zero, zero), unroll=4)
    return jnp.sum(a, 0, keepdims=True), jnp.sum(b, 0, keepdims=True)


ROOT = 0.7978845608028654


def gelu(u):
    return 0.5 * u * (1.0 + jnp.tanh(ROOT * (u + 0.044715 * (u * u * u))))


def gelu_slope(u):
    t = jnp.tanh(ROOT * (u + 0.044715 * (u * u * u)))
    return 0.5 * (1.0 + t) + 0.5 * u * (1.0 - t * t) * (ROOT * (1.0 + 0.134145 * (u * u)))


def pick(x, where, slot=15, count=64):
    lane = lax.broadcasted_iota(jnp.int32, (count, x.shape[1]), 1)
    row = lax.broadcasted_iota(jnp.int32, (count, x.shape[1]), 0)
    chosen = jnp.where(lane == row + where[slot] * count, 1.0, 0.0).astype(BF)
    return nt(chosen, x[...]).astype(BF)


def call(body, outs, scratch, args, specs, flops):
    return pl.pallas_call(
        body,
        out_shape=outs,
        in_specs=specs,
        out_specs=[VM] * len(outs),
        scratch_shapes=scratch,
        compiler_params=pltpu.CompilerParams(vmem_limit_bytes=58 * 1024 * 1024),
        cost_estimate=pl.CostEstimate(flops=flops, bytes_accessed=20_000_000, transcendentals=0),
    )(*args)


def s(shape, dtype):
    return jax.ShapeDtypeStruct(shape, dtype)


def head_probs(q, k, idk, idr, raw, probs, low):
    raw[...] = nt(k, q)
    for j in range(4):
        cols = slice(j * 128, j * 128 + 128)
        v = jnp.where(idk[...] == idr[:, cols], raw[:, cols] * (128**-0.5), -1e30)
        e = jnp.exp(v - jnp.max(v, 0, keepdims=True))
        p = e * (1.0 / jnp.sum(e, 0, keepdims=True))
        if probs is not None:
            probs[:, cols] = p
        low[:, cols] = p.astype(BF)


def lanes(h, base=0):
    return pl.ds(pl.multiple_of(base + h * 128, 128), 128)


def as_row(column):
    return jnp.broadcast_to(column, (512, 128)).T[0:1, :]


def layers(where, blend, rows, vecs, idk, idr, pixels, pl_low, folded, gain, segb, fours, groups, pieces):
    def body(where, blend, both, vecs, idk, idr, pixels, pl_low, folded, gain, segb, *refs):
        fours, refs = refs[:4], refs[4:]
        first, proj, second, refs = refs[:6], refs[6:8], refs[8:14], refs[14:]
        first_pieces, proj_pieces, second_pieces, refs = refs[:4], refs[4:8], refs[8:12], refs[12:]
        result, g1_own, grads_two, grads_proj, grads_one, small, pixel_grad, part, psum = refs[:9]
        w0, w1, w2, wp, one, pre, two, three, pre_two, dn, g, cross, low, act, att, att_grad, inner = refs[9:26]
        triple, dt, raw, probs, plow, slow, t_att, t_norm, t_act, t_low, t_self, sems = refs[26:]
        lat, cot = both.at[:, 0:1024], both.at[:, 1024:2048]
        own = pl.ds(pl.multiple_of(where[0] * 16, 16), 16)
        mix = blend[:, 0:CHANNELS]

        def fetch(dst, group, pieces, i, slot):
            return load(dst, where, group[i], group[i + 3], pieces, i, sems.at[slot])

        c0, c1, c2 = (fetch(w, first, first_pieces, i, i) for i, w in enumerate((w0, w1, w2)))
        cp = []
        for j in range(3):
            cp += load(wp, where, proj[0], proj[1], proj_pieces, j, sems.at[3 + j], 768, 256 * j)

        for i in range(4):
            cross[:, tile(where[1 + i])] = nn(mix, fours[i][288 : 288 + CHANNELS, :]).astype(BF)
        arrive(c0)

        def put(cols, acc):
            one[:, cols] = lat[:, cols].astype(F32) + acc

        by_cols(cross, w0, put)
        c0 = fetch(w0, second, second_pieces, 0, 6)
        t_att[...] = pick(cross, where)
        norm_into(low, one, vecs[1:2, :], vecs[5:6, :])
        arrive(c1)

        def put(cols, acc):
            u = acc + vecs[8:9, cols]
            pre[:, cols] = u
            act[:, cols] = gelu(u).astype(BF)

        by_cols(low, w1, put)
        c1 = fetch(w1, second, second_pieces, 1, 7)
        t_norm[...] = pick(low, where)
        arrive(c2)

        def put(cols, acc):
            two[:, cols] = one[:, cols] + (acc + vecs[9:10, cols])

        by_cols(act, w2, put)
        c2 = fetch(w2, second, second_pieces, 2, 8)
        t_act[...] = pick(act, where)

        norm_into(low, two, vecs[2:3, :], vecs[6:7, :])
        t_low[...] = pick(low, where)
        arrive(cp)

        def put(cols, acc):
            triple[:, cols] = acc.astype(BF)

        by_cols(low, wp, put)

        @pl.loop(0, HEADS // 2)
        def _(i):
            for p in range(2):
                h = 2 * i + p
                head_probs(triple[:, lanes(h)], triple[:, lanes(h, 1024)], idk, idr, raw.at[p], None, plow.at[p])
                att[:, lanes(h)] = tn(triple[:, lanes(h, 2048)], plow[p]).T.astype(BF)

        t_self[...] = pick(att, where)

        arrive(c0)

        def put(cols, acc):
            three[:, cols] = two[:, cols] + acc

        by_cols(att, w0, put)
        norm_into(low, three, vecs[3:4, :], vecs[7:8, :])
        arrive(c1)

        def put(cols, acc):
            u = acc + vecs[10:11, cols]
            pre_two[:, cols] = u
            act[:, cols] = gelu(u).astype(BF)

        by_cols(low, w1, put)
        arrive(c2)

        @pl.loop(0, 4)
        def _(j):
            acc = nn(act[own, :], w2[:, :, tile(j)].reshape(1024, 256)) + vecs[11:12, tile(j)]
            result[:, tile(j)] = (three[own, tile(j)] + acc).astype(BF)

        small[3:4, :] = jnp.sum(cot[...].astype(F32), 0, keepdims=True)
        grads_two[64:128, :] = nn(pick(act, where), cot[...]).astype(BF)

        def put(cols, acc):
            du = (acc * gelu_slope(pre_two[:, cols])).astype(BF)
            inner[:, cols] = du
            small[2:3, cols] = jnp.sum(du.astype(F32), 0, keepdims=True)

        by_rows(cot, w2, put)
        c2 = fetch(w2, first, first_pieces, 2, 9)
        grads_two[0:64, :] = nn(pick(low, where), inner[...]).astype(BF)

        def put(cols, acc):
            dn[:, cols] = acc

        by_rows(inner, w1, put)
        c1 = fetch(w1, first, first_pieces, 1, 10)
        da, db = norm_grad(g, low, three, vecs[3:4, :], dn, cot)
        small[0:1, :] = da
        small[1:2, :] = db
        grads_two[128:192, :] = nn(t_self[...], low[...]).astype(BF)

        def put(cols, acc):
            att_grad[:, cols] = acc.astype(BF)

        by_rows(low, w0, put)
        c0 = fetch(w0, first, first_pieces, 0, 11)

        scale = 128**-0.5

        @pl.loop(0, HEADS // 2)
        def _(i):
            for p in range(2):
                h = 2 * i + p
                q, k, v = (triple[:, lanes(h, b)] for b in (0, 1024, 2048))
                da = att_grad[:, lanes(h)]
                head_probs(q, k, idk, idr, raw.at[p], probs.at[p], plow.at[p])
                raw[p] = nt(v, da)
                for j in range(4):
                    cols = slice(j * 128, j * 128 + 128)
                    pr, dp = probs[p, :, cols], raw[p, :, cols]
                    slow[p, :, cols] = (pr * (dp - jnp.sum(pr * dp, 0, keepdims=True))).astype(BF)
                dt[:, lanes(h)] = (tn(k, slow[p]).T * scale).astype(BF)
                dt[:, lanes(h, 1024)] = (nn(slow[p], q) * scale).astype(BF)
                dt[:, lanes(h, 2048)] = nn(plow[p], da).astype(BF)

        for j in range(12):
            cols = slice(j * 256, j * 256 + 256)
            grads_proj[:, cols] = nn(t_low[...], dt[:, cols]).astype(BF)

        def put(cols, acc):
            dn[:, cols] = acc

        by_rows(dt, wp, put)
        da, db = norm_grad(g, low, two, vecs[2:3, :], dn, g)
        small[8:9, :] = da
        small[9:10, :] = db

        small[19:20, :] = jnp.sum(low[...].astype(F32), 0, keepdims=True)
        grads_one[64:128, :] = nn(t_act[...], low[...]).astype(BF)
        arrive(c2)

        def put(cols, acc):
            du = (acc * gelu_slope(pre[:, cols])).astype(BF)
            inner[:, cols] = du
            small[18:19, cols] = jnp.sum(du.astype(F32), 0, keepdims=True)

        by_rows(low, w2, put)
        grads_one[0:64, :] = nn(t_norm[...], inner[...]).astype(BF)
        arrive(c1)

        def put(cols, acc):
            dn[:, cols] = acc

        by_rows(inner, w1, put)
        da, db = norm_grad(g, low, one, vecs[1:2, :], dn, g)
        small[16:17, :] = da
        small[17:18, :] = db
        g1_own[...] = g[own, :]
        grads_one[128:192, :] = nn(t_att[...], low[...]).astype(BF)
        arrive(c0)

        def put(cols, acc):
            cross[:, cols] = acc.astype(BF)

        by_rows(low, w0, put)
        grads_one[192:224, :] = nn(pick(mix, where, 15, 32), cross[...]).astype(BF)
        total = nt(cross[:, tile(where[1])], fours[0][288 : 288 + CHANNELS, :])
        for i in range(1, 4):
            total += nt(cross[:, tile(where[1 + i])], fours[i][288 : 288 + CHANNELS, :])
        mix_grad = total.astype(BF)

        delta = as_row(jnp.sum(mix_grad.astype(F32) * mix.astype(F32), -1, keepdims=True))
        logs = as_row(jnp.sum(blend[:, CHANNELS : CHANNELS + 3].astype(F32), -1, keepdims=True))
        raw[0] = nt(pl_low[...], folded[...])
        raw[1] = nt(pl_low[...], mix_grad)
        for j in range(4):
            cols = slice(j * 128, j * 128 + 128)
            p = jnp.where(segb[...] == idr[:, cols], jnp.exp(raw[0, :, cols] - logs[:, cols]), 0.0)
            plow[0, :, cols] = p.astype(BF)
            slow[0, :, cols] = (p * (raw[1, :, cols] - delta[:, cols])).astype(BF)
        part[...] = (tn(pl_low[...], slow[0]).T * (1024**-0.5)).astype(BF)
        dn[:, 0:CHANNELS] = nn(slow[0], folded[...]) + nn(plow[0], mix_grad)

        def body(i, sums):
            rows = pl.ds(pl.multiple_of(i * STEP, STEP), STEP)
            hat, scale = norm_stats(pixels[rows, :].astype(F32))
            dy = dn[rows, 0:CHANNELS]
            dhat = dy * gain[...]
            back = scale * (
                dhat
                - jnp.mean(dhat, -1, keepdims=True)
                - hat * jnp.mean(dhat * hat, -1, keepdims=True)
            )
            pixel_grad[rows, :] = back.astype(BF)
            return sums[0] + jnp.sum(dy * hat, 0, keepdims=True), sums[1] + jnp.sum(dy, 0, keepdims=True)

        zero = jnp.zeros((1, CHANNELS), F32)
        a, b = lax.fori_loop(0, 512 // STEP, body, (zero, zero), unroll=4)
        psum[0:1, :] = a
        psum[1:2, :] = b

    return call(
        body,
        [
            s((16, 1024), BF),
            s((16, 1024), F32),
            s((192, 1024), BF),
            s((64, 3072), BF),
            s((224, 1024), BF),
            s((24, 1024), F32),
            s((512, CHANNELS), BF),
            s((512, CHANNELS), BF),
            s((2, CHANNELS), F32),
        ],
        [pltpu.VMEM((8, 128, 1024), BF)] * 3
        + [pltpu.VMEM((8, 128, 3072), BF)]
        + [pltpu.VMEM((512, 1024), F32)] * 7
        + [pltpu.VMEM((512, 1024), BF)] * 6
        + [pltpu.VMEM((512, 3072), BF)] * 2
        + [pltpu.VMEM((2, 512, 512), F32)] * 2
        + [pltpu.VMEM((2, 512, 512), BF)] * 2
        + [pltpu.VMEM((64, 512), BF)] * 5
        + [pltpu.SemaphoreType.DMA((12, 6))],
        (where, blend, rows, vecs, idk, idr, pixels, pl_low, folded, gain, segb, *fours, *groups, *pieces),
        [SM] + [VM] * 14 + [HBM] * 26,
        30_000_000_000,
    )


def front(where, lat, pixels, gain, bias, segb, idr, query_four, small_four):
    def body(where, rows, pixels, gain, bias, segb, idr, *refs):
        lat = rows.at[:, 0:1024]
        wq, fours, refs = refs[:4], refs[4:8], refs[8:]
        vecs, query, folded, pl_low, sent, tcross, low, raw, pt, turned = refs
        for k in range(4):
            vecs[:, tile(where[1 + k])] = fours[k][0:16, :].astype(F32)[0:12, :]
        norm_into(low, lat, vecs[0:1, :], vecs[4:5, :])

        @pl.loop(0, 512 // STEP, unroll=4)
        def _(i):
            rows = pl.ds(pl.multiple_of(i * STEP, STEP), STEP)
            hat, _ = norm_stats(pixels[rows, :].astype(F32))
            pl_low[rows, :] = (hat * gain[...] + bias[...]).astype(BF)

        total = None
        for k in range(4):
            cols = slice(k * 256, k * 256 + 256)
            query[:, cols] = nn(low[...], wq[k][...]).astype(BF)
            term = nt(query[:, cols], fours[k][16 : 16 + CHANNELS, :])
            total = term if total is None else total + term
        folded[...] = (total * (1024**-0.5)).astype(BF)
        raw[...] = nt(pl_low[...], folded[...])
        for j in range(4):
            cols = slice(j * 128, j * 128 + 128)
            allowed = segb[...] == idr[:, cols]
            v = jnp.where(allowed, raw[:, cols], -1e30)
            top = jnp.max(v, 0, keepdims=True)
            e = jnp.where(allowed, jnp.exp(v - top), 0.0)
            pt[:, cols] = e.astype(BF)
            weight = jnp.sum(e, 0, keepdims=True)
            some = weight > 0.0
            safe = jnp.where(some, weight, 1.0)
            logs = jnp.where(some, top + jnp.log(safe), -1e30)
            turned[0:CHANNELS, cols] = tn(pl_low[...], pt[:, cols]) * (1.0 / safe)
            high = logs.astype(BF).astype(F32)
            middle = (logs - high).astype(BF).astype(F32)
            turned[CHANNELS : CHANNELS + 1, cols] = high
            turned[CHANNELS + 1 : CHANNELS + 2, cols] = middle
            turned[CHANNELS + 2 : CHANNELS + 3, cols] = logs - high - middle
        sent[...] = turned[...].T.astype(BF)
        tcross[...] = pick(low, where, 0, 32)

    return call(
        body,
        [
            s((12, 1024), F32),
            s((512, 1024), BF),
            s((512, CHANNELS), BF),
            s((512, CHANNELS), BF),
            s((512, CHANNELS + 3), BF),
            s((32, 512), BF),
        ],
        [
            pltpu.VMEM((512, 1024), BF),
            pltpu.VMEM((512, 512), F32),
            pltpu.VMEM((512, 512), BF),
            pltpu.VMEM((CHANNELS + 3, 512), F32),
        ],
        (where, lat, pixels, gain, bias, segb, idr, *query_four, *small_four),
        [SM] + [VM] * 14,
        20_000_000_000,
    )


def finish(where, folded_grad, lat, vecs, tcross, query, g1_own, query_four, small_four):
    def body(where, folded_grad, rows, vecs, tcross, query, g1_own, *refs):
        lat = rows.at[:, 0:1024]
        wq, fours, refs = refs[:4], refs[4:8], refs[8:]
        latent, late, small, grad, dn = refs
        fg = folded_grad[...]
        for k in range(4):
            cols = slice(k * 256, k * 256 + 256)
            grad[:, cols] = nn(fg, fours[k][16 : 16 + CHANNELS, :]).astype(BF)
        for j in range(4):
            cols = slice(j * 256, j * 256 + 256)
            total = nt(grad[:, 0:256], wq[0][cols, :])
            for k in range(1, 4):
                total += nt(grad[:, k * 256 : k * 256 + 256], wq[k][cols, :])
            dn[:, cols] = total
        late[0:32, :] = nn(tcross[...], grad[...]).astype(BF)
        late[32:48, :] = nn(pick(fg, where, 0, 16), query[...]).astype(BF)

        def body(i, sums):
            rows = pl.ds(pl.multiple_of(i * STEP, STEP), STEP)
            hat, _ = norm_stats(lat[rows, :].astype(F32))
            dy = dn[rows, :]
            fold = lambda v: jnp.sum(v.reshape(STEP // 8, 8, 1024), 0)
            return sums[0] + fold(dy * hat), sums[1] + fold(dy)

        zero = jnp.zeros((8, 1024), F32)
        a, b = lax.fori_loop(0, 512 // STEP, body, (zero, zero), unroll=4)
        small[0:1, :] = jnp.sum(a, 0, keepdims=True)
        small[1:2, :] = jnp.sum(b, 0, keepdims=True)
        own = pl.ds(pl.multiple_of(where[0] * 16, 16), 16)
        hat, scale = norm_stats(lat[own, :].astype(F32))
        dhat = dn[own, :] * vecs[0:1, :]
        back = scale * (
            dhat
            - jnp.mean(dhat, -1, keepdims=True)
            - hat * jnp.mean(dhat * hat, -1, keepdims=True)
        )
        latent[...] = (g1_own[...] + back).astype(BF)

    return call(
        body,
        [s((16, 1024), BF), s((48, 1024), BF), s((2, 1024), F32)],
        [pltpu.VMEM((512, 1024), BF), pltpu.VMEM((512, 1024), F32)],
        (where, folded_grad, lat, vecs, tcross, query, g1_own, *query_four, *small_four),
        [SM] + [VM] * 14,
        2_500_000_000,
    )


def collect(where, cross, projection, later):
    def body(where, *refs):
        cross, projection, later, outs, sems = refs[:3], refs[3], refs[4:7], refs[7:10], refs[10]
        units = [(w, 0) for w in cross], [(projection, 256 * j) for j in range(3)], [(w, 0) for w in later]
        row = pl.multiple_of(where[14] * 512, 512)
        copies = []
        for g in range(3):
            for u, (w, col) in enumerate(units[g]):
                part = w.at[pl.ds(row, 512), pl.ds(col, 256)]
                copies.append(pltpu.make_async_copy(part, outs[g].at[u], sems.at[g, u]))
        for copy in copies:
            copy.start()
        arrive(copies)

    return pl.pallas_call(
        body,
        out_shape=[s((3, 512, 256), BF)] * 3,
        in_specs=[SM] + [HBM] * 7,
        out_specs=[VM] * 3,
        scratch_shapes=[pltpu.SemaphoreType.DMA((3, 3))],
        compiler_params=pltpu.CompilerParams(vmem_limit_bytes=58 * 1024 * 1024),
        cost_estimate=pl.CostEstimate(flops=0, bytes_accessed=4_800_000, transcendentals=0),
    )(where, *cross, projection, *later)


def settle(where, blocks, groups, shapes, places):
    def body(where, *refs):
        blocks, refs = refs[: len(refs) - 2 * len(shapes) - 1], refs[len(refs) - 2 * len(shapes) - 1 :]
        n = len(shapes)
        outs, bufs, sems = refs[:n], refs[n : 2 * n], refs[2 * n]
        copies = []
        last = [o for units in groups for o, _, _ in units]
        for units, where_from in zip(groups, places):
            base = 0
            for o, col, rows in units:
                short = shapes[o][0] == CHANNELS
                for which, index, place in where_from:
                    at = place(where)
                    if isinstance(at, int):
                        if short and at * rows >= CHANNELS:
                            continue
                        at = at * rows
                    else:
                        at = jnp.minimum(at, CHANNELS // rows + 1) if short else at
                        at = pl.multiple_of(at * rows, rows)
                    part = blocks[which][(*index, slice(base, base + rows))]
                    bufs[o][pl.ds(at, rows), col : col + 256] = part.astype(F32)
                base += rows
                last.pop(0)
                if short:
                    outs[o][...] = bufs[o][0:CHANNELS, :]
                elif o not in last:
                    copy = pltpu.make_async_copy(bufs[o], outs[o], sems.at[o])
                    copy.start()
                    copies.append(copy)
        arrive(copies)

    return pl.pallas_call(
        body,
        out_shape=[s(shape, F32) for shape in shapes],
        in_specs=[SM] + [VM] * len(blocks),
        out_specs=[VM if shape[0] == CHANNELS else HBM for shape in shapes],
        scratch_shapes=[pltpu.VMEM((320 if r == CHANNELS else r, c), F32) for r, c in shapes]
        + [pltpu.SemaphoreType.DMA((len(shapes),))],
        compiler_params=pltpu.CompilerParams(vmem_limit_bytes=58 * 1024 * 1024),
        cost_estimate=pl.CostEstimate(flops=0, bytes_accessed=10_000_000, transcendentals=0),
    )(where, *blocks)


def handed(x):
    def body(x, out):
        out[...] = x[...]

    return pl.pallas_call(
        body,
        out_shape=s(x.shape, x.dtype),
        in_specs=[VM],
        out_specs=VM,
        compiler_params=pltpu.CompilerParams(vmem_limit_bytes=58 * 1024 * 1024),
        cost_estimate=pl.CostEstimate(flops=20_000_000_000, bytes_accessed=1_000_000, transcendentals=0),
    )(x)


CTX = ("x", "zl", "y")
SHARD = ("zh", "core")


def shift(value, axis, by):
    count = lax.axis_size(axis)
    return lax.ppermute(value, axis, [(i, (i + by) % count) for i in range(count)])


def facing(value):
    return lax.ppermute(value, ("zl", "zh"), [(i, 3 - i) for i in range(4)])


def spread(rows):
    return lax.all_to_all(jnp.tile(rows, (32, 1)), CTX, 0, 0, tiled=True)


def in_three(value):
    high = lax.reduce_precision(value, 8, 7)
    rest = value - high
    middle = lax.reduce_precision(rest, 8, 7)
    return high.astype(BF), middle.astype(BF), (rest - middle).astype(BF)


def with_core(parts):
    return lax.ppermute(jnp.stack([parts[1], parts[3]]), SHARD, [(i, i ^ 1) for i in range(4)])


def with_facing(parts, got):
    near, far = parts[0].astype(F32) + got[0].astype(F32), parts[2].astype(F32) + got[1].astype(F32)
    return near, lax.ppermute(far.astype(BF), SHARD, [(i, i ^ 2) for i in range(4)])


def ring(rows, axis):
    return [rows] + [shift(rows, axis, k) for k in (1, 2, 3)]


def paired(rows, axis):
    two = jnp.stack([rows, lax.ppermute(rows, axis, [(i, i ^ 1) for i in range(4)])])
    return jnp.concatenate([two, lax.ppermute(two, axis, [(i, i ^ 3) for i in range(4)])])


def after(values, *events):
    return lax.optimization_barrier((values, events))[0]


def true_parts(block, own, width=256):
    rows = block.shape[0]
    return [lax.dynamic_slice(block, (0, (own ^ k) * width), (rows, width)) for k in range(4)]


def on_device(
    pixels,
    latents,
    input_segments,
    latent_offsets,
    pixel_gain,
    pixel_shift,
    query_weight,
    key_weight,
    value_weight,
    cross_output,
    cross_up,
    cross_down,
    self_projection,
    self_output,
    self_up,
    self_down,
    norm_gains,
    norm_shifts,
    dense_bias,
    cotangent,
):
    width = 1024
    channels = pixels.shape[2]
    ix, iy = lax.axis_index("x"), lax.axis_index("y")
    place = lax.axis_index(CTX)
    own = lax.axis_index(SHARD)
    where = jnp.stack(
        [place]
        + [own ^ k for k in range(4)]
        + [(ix + 4 - k) % 4 for k in range(4)]
        + [(iy + 4 - k) % 4 for k in range(4)]
        + [1 - lax.axis_index("zl"), lax.axis_index("zl")]
        + [ix * 4 + iy]
    ).astype(jnp.int32)

    small_own = jnp.concatenate(
        [
            norm_gains,
            norm_shifts,
            dense_bias,
            jnp.pad(key_weight, ((4, 272 - channels), (0, 0))),
            jnp.pad(value_weight, ((0, 272 - channels), (0, 0))),
        ],
        0,
    )
    both_rows = spread(jnp.concatenate([latents[0], cotangent[0]], 1))
    small_other, query_other = after((facing(small_own), facing(query_weight)), both_rows)
    small_four = [small_own, shift(small_own, "core", 1), small_other, shift(small_other, "core", 1)]
    query_four = [query_weight, shift(query_weight, "core", 1), query_other, shift(query_other, "core", 1)]

    where_now = after(where, small_own)
    send_one, send_proj, send_two = collect(
        where_now,
        [cross_output, cross_up, cross_down],
        self_projection,
        [self_output, self_up, self_down],
    )
    face_one = facing(send_one)

    def both(*weights):
        there = [shift(w, "core", 1) for w in weights]
        return [w.reshape(8, 128, -1) for w in (*weights, *there)]

    group_one = both(cross_output, cross_up, cross_down)
    group_proj = both(self_projection)
    group_two = both(self_output, self_up, self_down)

    ids = jnp.sum(
        (latent_offsets[0][None, 1:] <= jnp.arange(512, dtype=jnp.int32)[:, None]).astype(jnp.int32),
        1,
    )
    idk = jnp.broadcast_to(ids[:, None], (512, 128))
    idr = ids[None, :]

    segb = jnp.broadcast_to(input_segments[0][:, None], (512, 128))
    pgain, pbias = pixel_gain.astype(F32)[None], pixel_shift.astype(F32)[None]

    vecs, query, folded, pl_low, sent, tcross = front(
        where, after(both_rows, face_one), pixels[0], pgain, pbias, segb, idr, query_four, small_four
    )
    face_proj, face_two = facing(send_proj), facing(send_two)
    got = lax.all_to_all(sent, CTX, 0, 0, tiled=True)
    near_one = shift(after(face_one, sent), "zl", 1)
    near_proj = shift(after(face_proj, sent), "zl", 1)
    got = handed(after(got, near_one))
    got = got.astype(F32)
    got = got.reshape(32, 16, channels + 3)
    logs = jnp.sum(got[:, :, channels:], -1, keepdims=True)
    most = jnp.max(logs, 0, keepdims=True)
    share = jnp.exp(logs - most)
    share_sum = jnp.sum(share, 0)
    own_mixed = jnp.sum(share * got[:, :, :channels], 0) / share_sum
    own_log = most[0] + jnp.log(share_sum)
    packed = jnp.concatenate([own_mixed.astype(BF), *in_three(own_log)], 1)
    near_two = shift(after(face_two, got), "zl", 1)
    blend = handed(after(spread(packed), near_proj))

    def halves(face, near):
        pieces = [face, near, shift(face, "core", 1), shift(near, "core", 1)]
        return [piece.reshape(3, 4, 128, 256) for piece in pieces]

    result, g1_own, grads_two, grads_proj, grads_one, small_grads, pixel_grad, part, psum = layers(
        where, blend, both_rows, vecs, idk, idr, pixels[0], pl_low, folded, pgain, segb, small_four,
        (*group_one, *group_proj, *group_two),
        (*halves(face_one, near_one), *halves(face_proj, near_proj), *halves(face_two, near_two)),
    )
    small_two, small_proj, small_one = small_grads[:8], small_grads[8:16], small_grads[16:]

    parts = []
    for k in range(4):
        third = lax.dynamic_slice(grads_proj, (0, (own ^ k) * 768), (64, 768))
        thirds = [third[:, 256 * j : 256 * j + 256] for j in range(3)]
        at = (0, (own ^ k) * 256)
        parts.append(
            jnp.concatenate(
                [lax.dynamic_slice(grads_two, at, (192, 256)), *thirds, lax.dynamic_slice(grads_one, at, (224, 256))], 0
            )
        )
    got_core = with_core(parts)

    sums = jnp.stack(in_three(psum)).reshape(6, channels)
    sent = jnp.concatenate(
        [
            part.reshape(32, 16, channels),
            jnp.broadcast_to(sums[None], (32, 6, channels)),
        ],
        1,
    )
    got = jnp.sum(lax.all_to_all(sent, CTX, 0, 0, tiled=True).astype(F32), 0)
    pixel_sums = (got[16:18] + got[18:20]) + got[20:22]
    near, far = with_facing(parts, got_core)
    total = (near + far.astype(F32)).astype(BF)
    first, second = paired(total[:320], "x"), paired(total[320:], "y")
    own_folded = after(got[:16].astype(BF), first, second)
    beside = [shift(first, "y", 1), shift(first, "y", 3), shift(second, "x", 1), shift(second, "x", 3)]
    folded_grad = after(spread(own_folded), beside)
    far_first, far_second = after((first, second), folded_grad)
    first = [first, beside[0], shift(far_first, "y", 2), beside[1]]
    second = [second, beside[2], shift(far_second, "x", 2), beside[3]]
    latent_total, late, small_zero = finish(
        where, folded_grad, both_rows, vecs, tcross, query, g1_own, query_four, small_four
    )
    small = jnp.stack(
        [
            *(small_zero[0], small_one[0], small_proj[0], small_two[0]),
            *(small_zero[1], small_one[1], small_proj[1], small_two[1]),
            *(small_one[2], small_one[3], small_two[2], small_two[3]),
        ]
    ).astype(BF)

    def sixfold(value):
        parts = jnp.pad(jnp.concatenate(in_three(value), 0), ((0, 0), (0, 512 - channels)))
        return parts.reshape(12, 256)

    def whole(parts):
        return jnp.sum(parts.reshape(3, 2, 512).astype(F32), 0)[:, :channels]

    small_parts = true_parts(small, own)
    parts = [
        jnp.concatenate([late[:, 256 * k : 256 * k + 256], small_parts[k]], 0) for k in range(4)
    ]
    got = lax.ppermute(
        jnp.concatenate([parts[1], parts[3], sixfold(pixel_sums)], 0), SHARD, [(i, i ^ 1) for i in range(4)]
    )
    near = parts[0].astype(F32) + got[:60].astype(F32)
    far = parts[2].astype(F32) + got[60:120].astype(F32)
    pixel_sums = pixel_sums + whole(got[120:])
    got = lax.ppermute(
        jnp.concatenate([far.astype(BF), sixfold(pixel_sums)], 0), SHARD, [(i, i ^ 2) for i in range(4)]
    )
    late_sum = near + got[:60].astype(F32)
    norm_part = late_sum[48:60]
    pix = pixel_sums + whole(got[60:])

    last = spread(late_sum[:48].astype(BF)).reshape(32, 48, 256)
    tall, few = (1024, 256), (channels, 256)
    bits = (0, 1, 3, 2)
    su, sd, so, proj, cu, cd, co, v = settle(
        where,
        [*first, *second],
        [
            [(0, 0, 64), (1, 0, 64), (2, 0, 64), (3, 0, 64), (3, 256, 64)],
            [(3, 512, 64), (4, 0, 64), (5, 0, 64), (6, 0, 64), (7, 0, 32)],
        ],
        [tall, tall, tall, (1024, 768), tall, tall, tall, few],
        [
            [(k, (b,), lambda where, k=k, b=b: (where[5] ^ bits[b]) * 4 + where[9 + k]) for k in range(4) for b in range(4)],
            [(4 + k, (b,), lambda where, k=k, b=b: where[5 + k] * 4 + (where[9] ^ bits[b])) for k in range(4) for b in range(4)],
        ],
    )
    q, k = settle(
        where,
        [last],
        [[(0, 0, 32), (1, 0, 16)]],
        [tall, few],
        [[(0, (c,), lambda where, at=c: at) for c in range(32)]],
    )
    return (
        result[None],
        latent_total[None],
        pixel_grad[None],
        pix[0],
        pix[1],
        q,
        k,
        v,
        co,
        cu,
        cd,
        proj,
        so,
        su,
        sd,
        norm_part[:4],
        norm_part[4:8],
        norm_part[8:12],
    )


def solution(mesh):
    fine = Mesh(mesh.devices.reshape(4, 2, 4, 2, 2), CTX + SHARD)
    rows = P(SHARD, CTX, None)
    cols = P(None, SHARD)
    return jax.shard_map(
        on_device,
        mesh=fine,
        in_specs=(
            rows,
            rows,
            P(SHARD, CTX),
            P(SHARD, None),
            P(),
            P(),
            *([cols] * 13),
            rows,
        ),
        out_specs=(rows, rows, rows, P(), P(), *([cols] * 13)),
        check_vma=False,
    )
```

```python
import jax
import jax.numpy as jnp
from jax import lax
from jax.experimental import pallas as pl
from jax.experimental.pallas import tpu as pltpu
from jax.sharding import Mesh, PartitionSpec as P

BF = jnp.bfloat16
F32 = jnp.float32
HEADS = 8
CHANNELS = 261
HBM = pl.BlockSpec(memory_space=pl.ANY)
VM = pl.BlockSpec(memory_space=pltpu.VMEM)
SM = pl.BlockSpec(memory_space=pltpu.SMEM)
STEP = 64


def nn(a, b):
    return lax.dot_general(a, b, (((1,), (0,)), ((), ())), preferred_element_type=F32)


def nt(a, b):
    return lax.dot_general(a, b, (((1,), (1,)), ((), ())), preferred_element_type=F32)


def tn(a, b):
    return lax.dot_general(a, b, (((0,), (0,)), ((), ())), preferred_element_type=F32)


def tile(j):
    return pl.ds(pl.multiple_of(j * 256, 256), 256)


def load(dst, where, own, there, pieces, unit, sems, width=256, offset=0):
    copies = []

    def go(part, rows, slot):
        at = pl.multiple_of(where[slot] * width + offset, 256)
        copy = pltpu.make_async_copy(part, dst.at[rows, :, pl.ds(at, 256)], sems.at[len(copies)])
        copy.start()
        copies.append(copy)

    cols = pl.ds(offset, 256)
    go(own.at[:, :, cols], pl.ds(0, 8), 1)
    go(there.at[:, :, cols], pl.ds(0, 8), 2)
    for k in range(4):
        go(pieces[k].at[unit], pl.ds(4 * where[13 + k % 2], 4), 3 + k // 2)
    return copies


def arrive(copies):
    for copy in copies:
        copy.wait()


def by_cols(x, w, then):
    for j in range(w.shape[2] // 256):
        cols = slice(j * 256, j * 256 + 256)
        then(cols, nn(x[...], w[:, :, cols].reshape(1024, 256)))


def by_rows(dy, w, then):
    for j in range(4):
        block = w[2 * j : 2 * j + 2].reshape(256, w.shape[2])
        then(slice(j * 256, j * 256 + 256), nt(dy[...], block))


def norm_stats(v):
    center = jnp.mean(v, -1, keepdims=True)
    centred = v - center
    scale = lax.rsqrt(jnp.mean(centred * centred, -1, keepdims=True) + 1e-05)
    return centred * scale, scale


def norm_into(out, stream, gain, bias):
    @pl.loop(0, 512 // STEP, unroll=4)
    def _(i):
        rows = pl.ds(pl.multiple_of(i * STEP, STEP), STEP)
        hat, _ = norm_stats(stream[rows, :].astype(F32))
        out[rows, :] = (hat * gain + bias).astype(BF)


def norm_grad(out, low, stream, gain, grad, carry):
    def body(i, sums):
        rows = pl.ds(pl.multiple_of(i * STEP, STEP), STEP)
        hat, scale = norm_stats(stream[rows, :])
        dy = grad[rows, :]
        dhat = dy * gain
        back = scale * (
            dhat
            - jnp.mean(dhat, -1, keepdims=True)
            - hat * jnp.mean(dhat * hat, -1, keepdims=True)
        )
        new = carry[rows, :].astype(F32) + back
        out[rows, :] = new
        low[rows, :] = new.astype(BF)
        fold = lambda v: jnp.sum(v.reshape(STEP // 8, 8, 1024), 0)
        return sums[0] + fold(dy * hat), sums[1] + fold(dy)

    zero = jnp.zeros((8, 1024), F32)
    a, b = lax.fori_loop(0, 512 // STEP, body, (zero, zero), unroll=4)
    return jnp.sum(a, 0, keepdims=True), jnp.sum(b, 0, keepdims=True)


ROOT = 0.7978845608028654


def gelu(u):
    return 0.5 * u * (1.0 + jnp.tanh(ROOT * (u + 0.044715 * (u * u * u))))


def gelu_slope(u):
    t = jnp.tanh(ROOT * (u + 0.044715 * (u * u * u)))
    return 0.5 * (1.0 + t) + 0.5 * u * (1.0 - t * t) * (ROOT * (1.0 + 0.134145 * (u * u)))


def pick(x, where, slot=15, count=64):
    lane = lax.broadcasted_iota(jnp.int32, (count, x.shape[1]), 1)
    row = lax.broadcasted_iota(jnp.int32, (count, x.shape[1]), 0)
    chosen = jnp.where(lane == row + where[slot] * count, 1.0, 0.0).astype(BF)
    return nt(chosen, x[...]).astype(BF)


def call(body, outs, scratch, args, specs, flops):
    return pl.pallas_call(
        body,
        out_shape=outs,
        in_specs=specs,
        out_specs=[VM] * len(outs),
        scratch_shapes=scratch,
        compiler_params=pltpu.CompilerParams(vmem_limit_bytes=58 * 1024 * 1024),
        cost_estimate=pl.CostEstimate(flops=flops, bytes_accessed=20_000_000, transcendentals=0),
    )(*args)


def s(shape, dtype):
    return jax.ShapeDtypeStruct(shape, dtype)


def head_probs(q, k, idk, idr, raw, probs, low):
    raw[...] = nt(k, q)
    for j in range(4):
        cols = slice(j * 128, j * 128 + 128)
        v = jnp.where(idk[...] == idr[:, cols], raw[:, cols] * (128**-0.5), -1e30)
        e = jnp.exp(v - jnp.max(v, 0, keepdims=True))
        p = e * (1.0 / jnp.sum(e, 0, keepdims=True))
        if probs is not None:
            probs[:, cols] = p
        low[:, cols] = p.astype(BF)


def lanes(h, base=0):
    return pl.ds(pl.multiple_of(base + h * 128, 128), 128)


def as_row(column):
    return jnp.broadcast_to(column, (512, 128)).T[0:1, :]


def layers(where, blend, rows, vecs, idk, idr, pixels, pl_low, folded, gain, segb, fours, groups, pieces):
    def body(where, blend, both, vecs, idk, idr, pixels, pl_low, folded, gain, segb, *refs):
        fours, refs = refs[:4], refs[4:]
        first, proj, second, refs = refs[:6], refs[6:8], refs[8:14], refs[14:]
        first_pieces, proj_pieces, second_pieces, refs = refs[:4], refs[4:8], refs[8:12], refs[12:]
        result, g1_own, grads_two, grads_proj, grads_one, small, pixel_grad, part, psum = refs[:9]
        w0, w1, w2, wp, one, pre, two, three, pre_two, dn, g, cross, low, act, att, att_grad, inner = refs[9:26]
        triple, dt, raw, probs, plow, slow, t_att, t_norm, t_act, t_low, t_self, sems = refs[26:]
        lat, cot = both.at[:, 0:1024], both.at[:, 1024:2048]
        own = pl.ds(pl.multiple_of(where[0] * 16, 16), 16)
        mix = blend[:, 0:CHANNELS]

        def fetch(dst, group, pieces, i, slot):
            return load(dst, where, group[i], group[i + 3], pieces, i, sems.at[slot])

        c0, c1, c2 = (fetch(w, first, first_pieces, i, i) for i, w in enumerate((w0, w1, w2)))
        cp = []
        for j in range(3):
            cp += load(wp, where, proj[0], proj[1], proj_pieces, j, sems.at[3 + j], 768, 256 * j)

        for i in range(4):
            cross[:, tile(where[1 + i])] = nn(mix, fours[i][288 : 288 + CHANNELS, :]).astype(BF)
        arrive(c0)

        def put(cols, acc):
            one[:, cols] = lat[:, cols].astype(F32) + acc

        by_cols(cross, w0, put)
        c0 = fetch(w0, second, second_pieces, 0, 6)
        t_att[...] = pick(cross, where)
        norm_into(low, one, vecs[1:2, :], vecs[5:6, :])
        arrive(c1)

        def put(cols, acc):
            u = acc + vecs[8:9, cols]
            pre[:, cols] = u
            act[:, cols] = gelu(u).astype(BF)

        by_cols(low, w1, put)
        c1 = fetch(w1, second, second_pieces, 1, 7)
        t_norm[...] = pick(low, where)
        arrive(c2)

        def put(cols, acc):
            two[:, cols] = one[:, cols] + (acc + vecs[9:10, cols])

        by_cols(act, w2, put)
        c2 = fetch(w2, second, second_pieces, 2, 8)
        t_act[...] = pick(act, where)

        norm_into(low, two, vecs[2:3, :], vecs[6:7, :])
        t_low[...] = pick(low, where)
        arrive(cp)

        def put(cols, acc):
            triple[:, cols] = acc.astype(BF)

        by_cols(low, wp, put)

        @pl.loop(0, HEADS // 2)
        def _(i):
            for p in range(2):
                h = 2 * i + p
                head_probs(triple[:, lanes(h)], triple[:, lanes(h, 1024)], idk, idr, raw.at[p], None, plow.at[p])
                att[:, lanes(h)] = tn(triple[:, lanes(h, 2048)], plow[p]).T.astype(BF)

        t_self[...] = pick(att, where)

        arrive(c0)

        def put(cols, acc):
            three[:, cols] = two[:, cols] + acc

        by_cols(att, w0, put)
        norm_into(low, three, vecs[3:4, :], vecs[7:8, :])
        arrive(c1)

        def put(cols, acc):
            u = acc + vecs[10:11, cols]
            pre_two[:, cols] = u
            act[:, cols] = gelu(u).astype(BF)

        by_cols(low, w1, put)
        arrive(c2)

        @pl.loop(0, 4)
        def _(j):
            acc = nn(act[own, :], w2[:, :, tile(j)].reshape(1024, 256)) + vecs[11:12, tile(j)]
            result[:, tile(j)] = (three[own, tile(j)] + acc).astype(BF)

        small[3:4, :] = jnp.sum(cot[...].astype(F32), 0, keepdims=True)
        grads_two[64:128, :] = nn(pick(act, where), cot[...]).astype(BF)

        def put(cols, acc):
            du = (acc * gelu_slope(pre_two[:, cols])).astype(BF)
            inner[:, cols] = du
            small[2:3, cols] = jnp.sum(du.astype(F32), 0, keepdims=True)

        by_rows(cot, w2, put)
        c2 = fetch(w2, first, first_pieces, 2, 9)
        grads_two[0:64, :] = nn(pick(low, where), inner[...]).astype(BF)

        def put(cols, acc):
            dn[:, cols] = acc

        by_rows(inner, w1, put)
        c1 = fetch(w1, first, first_pieces, 1, 10)
        da, db = norm_grad(g, low, three, vecs[3:4, :], dn, cot)
        small[0:1, :] = da
        small[1:2, :] = db
        grads_two[128:192, :] = nn(t_self[...], low[...]).astype(BF)

        def put(cols, acc):
            att_grad[:, cols] = acc.astype(BF)

        by_rows(low, w0, put)
        c0 = fetch(w0, first, first_pieces, 0, 11)

        scale = 128**-0.5

        @pl.loop(0, HEADS // 2)
        def _(i):
            for p in range(2):
                h = 2 * i + p
                q, k, v = (triple[:, lanes(h, b)] for b in (0, 1024, 2048))
                da = att_grad[:, lanes(h)]
                head_probs(q, k, idk, idr, raw.at[p], probs.at[p], plow.at[p])
                raw[p] = nt(v, da)
                for j in range(4):
                    cols = slice(j * 128, j * 128 + 128)
                    pr, dp = probs[p, :, cols], raw[p, :, cols]
                    slow[p, :, cols] = (pr * (dp - jnp.sum(pr * dp, 0, keepdims=True))).astype(BF)
                dt[:, lanes(h)] = (tn(k, slow[p]).T * scale).astype(BF)
                dt[:, lanes(h, 1024)] = (nn(slow[p], q) * scale).astype(BF)
                dt[:, lanes(h, 2048)] = nn(plow[p], da).astype(BF)

        for j in range(12):
            cols = slice(j * 256, j * 256 + 256)
            grads_proj[:, cols] = nn(t_low[...], dt[:, cols]).astype(BF)

        def put(cols, acc):
            dn[:, cols] = acc

        by_rows(dt, wp, put)
        da, db = norm_grad(g, low, two, vecs[2:3, :], dn, g)
        small[8:9, :] = da
        small[9:10, :] = db

        small[19:20, :] = jnp.sum(low[...].astype(F32), 0, keepdims=True)
        grads_one[64:128, :] = nn(t_act[...], low[...]).astype(BF)
        arrive(c2)

        def put(cols, acc):
            du = (acc * gelu_slope(pre[:, cols])).astype(BF)
            inner[:, cols] = du
            small[18:19, cols] = jnp.sum(du.astype(F32), 0, keepdims=True)

        by_rows(low, w2, put)
        grads_one[0:64, :] = nn(t_norm[...], inner[...]).astype(BF)
        arrive(c1)

        def put(cols, acc):
            dn[:, cols] = acc

        by_rows(inner, w1, put)
        da, db = norm_grad(g, low, one, vecs[1:2, :], dn, g)
        small[16:17, :] = da
        small[17:18, :] = db
        g1_own[...] = g[own, :]
        grads_one[128:192, :] = nn(t_att[...], low[...]).astype(BF)
        arrive(c0)

        def put(cols, acc):
            cross[:, cols] = acc.astype(BF)

        by_rows(low, w0, put)
        grads_one[192:224, :] = nn(pick(mix, where, 15, 32), cross[...]).astype(BF)
        total = nt(cross[:, tile(where[1])], fours[0][288 : 288 + CHANNELS, :])
        for i in range(1, 4):
            total += nt(cross[:, tile(where[1 + i])], fours[i][288 : 288 + CHANNELS, :])
        mix_grad = total.astype(BF)

        delta = as_row(jnp.sum(mix_grad.astype(F32) * mix.astype(F32), -1, keepdims=True))
        logs = as_row(jnp.sum(blend[:, CHANNELS : CHANNELS + 3].astype(F32), -1, keepdims=True))
        raw[0] = nt(pl_low[...], folded[...])
        raw[1] = nt(pl_low[...], mix_grad)
        for j in range(4):
            cols = slice(j * 128, j * 128 + 128)
            p = jnp.where(segb[...] == idr[:, cols], jnp.exp(raw[0, :, cols] - logs[:, cols]), 0.0)
            plow[0, :, cols] = p.astype(BF)
            slow[0, :, cols] = (p * (raw[1, :, cols] - delta[:, cols])).astype(BF)
        part[...] = (tn(pl_low[...], slow[0]).T * (1024**-0.5)).astype(BF)
        dn[:, 0:CHANNELS] = nn(slow[0], folded[...]) + nn(plow[0], mix_grad)

        def body(i, sums):
            rows = pl.ds(pl.multiple_of(i * STEP, STEP), STEP)
            hat, scale = norm_stats(pixels[rows, :].astype(F32))
            dy = dn[rows, 0:CHANNELS]
            dhat = dy * gain[...]
            back = scale * (
                dhat
                - jnp.mean(dhat, -1, keepdims=True)
                - hat * jnp.mean(dhat * hat, -1, keepdims=True)
            )
            pixel_grad[rows, :] = back.astype(BF)
            return sums[0] + jnp.sum(dy * hat, 0, keepdims=True), sums[1] + jnp.sum(dy, 0, keepdims=True)

        zero = jnp.zeros((1, CHANNELS), F32)
        a, b = lax.fori_loop(0, 512 // STEP, body, (zero, zero), unroll=4)
        psum[0:1, :] = a
        psum[1:2, :] = b

    return call(
        body,
        [
            s((16, 1024), BF),
            s((16, 1024), F32),
            s((192, 1024), BF),
            s((64, 3072), BF),
            s((224, 1024), BF),
            s((24, 1024), F32),
            s((512, CHANNELS), BF),
            s((512, CHANNELS), BF),
            s((2, CHANNELS), F32),
        ],
        [pltpu.VMEM((8, 128, 1024), BF)] * 3
        + [pltpu.VMEM((8, 128, 3072), BF)]
        + [pltpu.VMEM((512, 1024), F32)] * 7
        + [pltpu.VMEM((512, 1024), BF)] * 6
        + [pltpu.VMEM((512, 3072), BF)] * 2
        + [pltpu.VMEM((2, 512, 512), F32)] * 2
        + [pltpu.VMEM((2, 512, 512), BF)] * 2
        + [pltpu.VMEM((64, 512), BF)] * 5
        + [pltpu.SemaphoreType.DMA((12, 6))],
        (where, blend, rows, vecs, idk, idr, pixels, pl_low, folded, gain, segb, *fours, *groups, *pieces),
        [SM] + [VM] * 14 + [HBM] * 26,
        30_000_000_000,
    )


def front(where, lat, pixels, gain, bias, segb, idr, query_four, small_four):
    def body(where, rows, pixels, gain, bias, segb, idr, *refs):
        lat = rows.at[:, 0:1024]
        wq, fours, refs = refs[:4], refs[4:8], refs[8:]
        vecs, query, folded, pl_low, sent, tcross, low, raw, pt, turned = refs
        for k in range(4):
            vecs[:, tile(where[1 + k])] = fours[k][0:16, :].astype(F32)[0:12, :]
        norm_into(low, lat, vecs[0:1, :], vecs[4:5, :])

        @pl.loop(0, 512 // STEP, unroll=4)
        def _(i):
            rows = pl.ds(pl.multiple_of(i * STEP, STEP), STEP)
            hat, _ = norm_stats(pixels[rows, :].astype(F32))
            pl_low[rows, :] = (hat * gain[...] + bias[...]).astype(BF)

        total = None
        for k in range(4):
            cols = slice(k * 256, k * 256 + 256)
            query[:, cols] = nn(low[...], wq[k][...]).astype(BF)
            term = nt(query[:, cols], fours[k][16 : 16 + CHANNELS, :])
            total = term if total is None else total + term
        folded[...] = (total * (1024**-0.5)).astype(BF)
        raw[...] = nt(pl_low[...], folded[...])
        for j in range(4):
            cols = slice(j * 128, j * 128 + 128)
            allowed = segb[...] == idr[:, cols]
            v = jnp.where(allowed, raw[:, cols], -1e30)
            top = jnp.max(v, 0, keepdims=True)
            e = jnp.where(allowed, jnp.exp(v - top), 0.0)
            pt[:, cols] = e.astype(BF)
            weight = jnp.sum(e, 0, keepdims=True)
            some = weight > 0.0
            safe = jnp.where(some, weight, 1.0)
            logs = jnp.where(some, top + jnp.log(safe), -1e30)
            turned[0:CHANNELS, cols] = tn(pl_low[...], pt[:, cols]) * (1.0 / safe)
            high = logs.astype(BF).astype(F32)
            middle = (logs - high).astype(BF).astype(F32)
            turned[CHANNELS : CHANNELS + 1, cols] = high
            turned[CHANNELS + 1 : CHANNELS + 2, cols] = middle
            turned[CHANNELS + 2 : CHANNELS + 3, cols] = logs - high - middle
        sent[...] = turned[...].T.astype(BF)
        tcross[...] = pick(low, where, 0, 32)

    return call(
        body,
        [
            s((12, 1024), F32),
            s((512, 1024), BF),
            s((512, CHANNELS), BF),
            s((512, CHANNELS), BF),
            s((512, CHANNELS + 3), BF),
            s((32, 512), BF),
        ],
        [
            pltpu.VMEM((512, 1024), BF),
            pltpu.VMEM((512, 512), F32),
            pltpu.VMEM((512, 512), BF),
            pltpu.VMEM((CHANNELS + 3, 512), F32),
        ],
        (where, lat, pixels, gain, bias, segb, idr, *query_four, *small_four),
        [SM] + [VM] * 14,
        20_000_000_000,
    )


def finish(where, folded_grad, lat, vecs, tcross, query, g1_own, query_four, small_four):
    def body(where, folded_grad, rows, vecs, tcross, query, g1_own, *refs):
        lat = rows.at[:, 0:1024]
        wq, fours, refs = refs[:4], refs[4:8], refs[8:]
        latent, late, small, grad, dn = refs
        fg = folded_grad[...]
        for k in range(4):
            cols = slice(k * 256, k * 256 + 256)
            grad[:, cols] = nn(fg, fours[k][16 : 16 + CHANNELS, :]).astype(BF)
        for j in range(4):
            cols = slice(j * 256, j * 256 + 256)
            total = nt(grad[:, 0:256], wq[0][cols, :])
            for k in range(1, 4):
                total += nt(grad[:, k * 256 : k * 256 + 256], wq[k][cols, :])
            dn[:, cols] = total
        late[0:32, :] = nn(tcross[...], grad[...]).astype(BF)
        late[32:48, :] = nn(pick(fg, where, 0, 16), query[...]).astype(BF)

        def body(i, sums):
            rows = pl.ds(pl.multiple_of(i * STEP, STEP), STEP)
            hat, _ = norm_stats(lat[rows, :].astype(F32))
            dy = dn[rows, :]
            fold = lambda v: jnp.sum(v.reshape(STEP // 8, 8, 1024), 0)
            return sums[0] + fold(dy * hat), sums[1] + fold(dy)

        zero = jnp.zeros((8, 1024), F32)
        a, b = lax.fori_loop(0, 512 // STEP, body, (zero, zero), unroll=4)
        small[0:1, :] = jnp.sum(a, 0, keepdims=True)
        small[1:2, :] = jnp.sum(b, 0, keepdims=True)
        own = pl.ds(pl.multiple_of(where[0] * 16, 16), 16)
        hat, scale = norm_stats(lat[own, :].astype(F32))
        dhat = dn[own, :] * vecs[0:1, :]
        back = scale * (
            dhat
            - jnp.mean(dhat, -1, keepdims=True)
            - hat * jnp.mean(dhat * hat, -1, keepdims=True)
        )
        latent[...] = (g1_own[...] + back).astype(BF)

    return call(
        body,
        [s((16, 1024), BF), s((48, 1024), BF), s((2, 1024), F32)],
        [pltpu.VMEM((512, 1024), BF), pltpu.VMEM((512, 1024), F32)],
        (where, folded_grad, lat, vecs, tcross, query, g1_own, *query_four, *small_four),
        [SM] + [VM] * 14,
        2_500_000_000,
    )


def collect(where, cross, projection, later):
    def body(where, *refs):
        cross, projection, later, outs, sems = refs[:3], refs[3], refs[4:7], refs[7:10], refs[10]
        units = [(w, 0) for w in cross], [(projection, 256 * j) for j in range(3)], [(w, 0) for w in later]
        row = pl.multiple_of(where[14] * 512, 512)
        copies = []
        for g in range(3):
            for u, (w, col) in enumerate(units[g]):
                part = w.at[pl.ds(row, 512), pl.ds(col, 256)]
                copies.append(pltpu.make_async_copy(part, outs[g].at[u], sems.at[g, u]))
        for copy in copies:
            copy.start()
        arrive(copies)

    return pl.pallas_call(
        body,
        out_shape=[s((3, 512, 256), BF)] * 3,
        in_specs=[SM] + [HBM] * 7,
        out_specs=[VM] * 3,
        scratch_shapes=[pltpu.SemaphoreType.DMA((3, 3))],
        compiler_params=pltpu.CompilerParams(vmem_limit_bytes=58 * 1024 * 1024),
        cost_estimate=pl.CostEstimate(flops=0, bytes_accessed=4_800_000, transcendentals=0),
    )(where, *cross, projection, *later)


def settle(where, blocks, groups, shapes, places):
    def body(where, *refs):
        blocks, refs = refs[: len(refs) - 2 * len(shapes) - 1], refs[len(refs) - 2 * len(shapes) - 1 :]
        n = len(shapes)
        outs, bufs, sems = refs[:n], refs[n : 2 * n], refs[2 * n]
        copies = []
        last = [o for units in groups for o, _, _ in units]
        for units, where_from in zip(groups, places):
            base = 0
            for o, col, rows in units:
                short = shapes[o][0] == CHANNELS
                for which, index, place in where_from:
                    at = place(where)
                    if isinstance(at, int):
                        if short and at * rows >= CHANNELS:
                            continue
                        at = at * rows
                    else:
                        at = jnp.minimum(at, CHANNELS // rows + 1) if short else at
                        at = pl.multiple_of(at * rows, rows)
                    part = blocks[which][(*index, slice(base, base + rows))]
                    bufs[o][pl.ds(at, rows), col : col + 256] = part.astype(F32)
                base += rows
                last.pop(0)
                if short:
                    outs[o][...] = bufs[o][0:CHANNELS, :]
                elif o not in last:
                    copy = pltpu.make_async_copy(bufs[o], outs[o], sems.at[o])
                    copy.start()
                    copies.append(copy)
        arrive(copies)

    return pl.pallas_call(
        body,
        out_shape=[s(shape, F32) for shape in shapes],
        in_specs=[SM] + [VM] * len(blocks),
        out_specs=[VM if shape[0] == CHANNELS else HBM for shape in shapes],
        scratch_shapes=[pltpu.VMEM((320 if r == CHANNELS else r, c), F32) for r, c in shapes]
        + [pltpu.SemaphoreType.DMA((len(shapes),))],
        compiler_params=pltpu.CompilerParams(vmem_limit_bytes=58 * 1024 * 1024),
        cost_estimate=pl.CostEstimate(flops=0, bytes_accessed=10_000_000, transcendentals=0),
    )(where, *blocks)


def handed(x):
    def body(x, out):
        out[...] = x[...]

    return pl.pallas_call(
        body,
        out_shape=s(x.shape, x.dtype),
        in_specs=[VM],
        out_specs=VM,
        compiler_params=pltpu.CompilerParams(vmem_limit_bytes=58 * 1024 * 1024),
        cost_estimate=pl.CostEstimate(flops=20_000_000_000, bytes_accessed=1_000_000, transcendentals=0),
    )(x)


CTX = ("x", "zl", "y")
SHARD = ("zh", "core")


def shift(value, axis, by):
    count = lax.axis_size(axis)
    return lax.ppermute(value, axis, [(i, (i + by) % count) for i in range(count)])


def facing(value):
    return lax.ppermute(value, ("zl", "zh"), [(i, 3 - i) for i in range(4)])


def spread(rows):
    return lax.all_to_all(jnp.tile(rows, (32, 1)), CTX, 0, 0, tiled=True)


def in_three(value):
    high = lax.reduce_precision(value, 8, 7)
    rest = value - high
    middle = lax.reduce_precision(rest, 8, 7)
    return high.astype(BF), middle.astype(BF), (rest - middle).astype(BF)


def with_core(parts):
    return lax.ppermute(jnp.stack([parts[1], parts[3]]), SHARD, [(i, i ^ 1) for i in range(4)])


def with_facing(parts, got):
    near, far = parts[0].astype(F32) + got[0].astype(F32), parts[2].astype(F32) + got[1].astype(F32)
    return near, lax.ppermute(far.astype(BF), SHARD, [(i, i ^ 2) for i in range(4)])


def ring(rows, axis):
    return [rows] + [shift(rows, axis, k) for k in (1, 2, 3)]


def paired(rows, axis):
    two = jnp.stack([rows, lax.ppermute(rows, axis, [(i, i ^ 1) for i in range(4)])])
    return jnp.concatenate([two, lax.ppermute(two, axis, [(i, i ^ 3) for i in range(4)])])


def after(values, *events):
    return lax.optimization_barrier((values, events))[0]


def true_parts(block, own, width=256):
    rows = block.shape[0]
    return [lax.dynamic_slice(block, (0, (own ^ k) * width), (rows, width)) for k in range(4)]


def on_device(
    pixels,
    latents,
    input_segments,
    latent_offsets,
    pixel_gain,
    pixel_shift,
    query_weight,
    key_weight,
    value_weight,
    cross_output,
    cross_up,
    cross_down,
    self_projection,
    self_output,
    self_up,
    self_down,
    norm_gains,
    norm_shifts,
    dense_bias,
    cotangent,
):
    width = 1024
    channels = pixels.shape[2]
    ix, iy = lax.axis_index("x"), lax.axis_index("y")
    place = lax.axis_index(CTX)
    own = lax.axis_index(SHARD)
    where = jnp.stack(
        [place]
        + [own ^ k for k in range(4)]
        + [(ix + 4 - k) % 4 for k in range(4)]
        + [(iy + 4 - k) % 4 for k in range(4)]
        + [1 - lax.axis_index("zl"), lax.axis_index("zl")]
        + [ix * 4 + iy]
    ).astype(jnp.int32)

    small_own = jnp.concatenate(
        [
            norm_gains,
            norm_shifts,
            dense_bias,
            jnp.pad(key_weight, ((4, 272 - channels), (0, 0))),
            jnp.pad(value_weight, ((0, 272 - channels), (0, 0))),
        ],
        0,
    )
    both_rows = spread(jnp.concatenate([latents[0], cotangent[0]], 1))
    small_other, query_other = after((facing(small_own), facing(query_weight)), both_rows)
    small_four = [small_own, shift(small_own, "core", 1), small_other, shift(small_other, "core", 1)]
    query_four = [query_weight, shift(query_weight, "core", 1), query_other, shift(query_other, "core", 1)]

    where_now = after(where, small_own)
    send_one, send_proj, send_two = collect(
        where_now,
        [cross_output, cross_up, cross_down],
        self_projection,
        [self_output, self_up, self_down],
    )
    face_one = facing(send_one)

    def both(*weights):
        there = [shift(w, "core", 1) for w in weights]
        return [w.reshape(8, 128, -1) for w in (*weights, *there)]

    group_one = both(cross_output, cross_up, cross_down)
    group_proj = both(self_projection)
    group_two = both(self_output, self_up, self_down)

    ids = jnp.sum(
        (latent_offsets[0][None, 1:] <= jnp.arange(512, dtype=jnp.int32)[:, None]).astype(jnp.int32),
        1,
    )
    idk = jnp.broadcast_to(ids[:, None], (512, 128))
    idr = ids[None, :]

    segb = jnp.broadcast_to(input_segments[0][:, None], (512, 128))
    pgain, pbias = pixel_gain.astype(F32)[None], pixel_shift.astype(F32)[None]

    vecs, query, folded, pl_low, sent, tcross = front(
        where, after(both_rows, face_one), pixels[0], pgain, pbias, segb, idr, query_four, small_four
    )
    face_proj, face_two = facing(send_proj), facing(send_two)
    got = lax.all_to_all(sent, CTX, 0, 0, tiled=True)
    near_one = shift(after(face_one, sent), "zl", 1)
    near_proj = shift(after(face_proj, sent), "zl", 1)
    got = handed(after(got, near_one))
    got = got.astype(F32)
    got = got.reshape(32, 16, channels + 3)
    logs = jnp.sum(got[:, :, channels:], -1, keepdims=True)
    most = jnp.max(logs, 0, keepdims=True)
    share = jnp.exp(logs - most)
    share_sum = jnp.sum(share, 0)
    own_mixed = jnp.sum(share * got[:, :, :channels], 0) / share_sum
    own_log = most[0] + jnp.log(share_sum)
    packed = jnp.concatenate([own_mixed.astype(BF), *in_three(own_log)], 1)
    near_two = shift(after(face_two, got), "zl", 1)
    blend = handed(after(spread(packed), near_proj))

    def halves(face, near):
        pieces = [face, near, shift(face, "core", 1), shift(near, "core", 1)]
        return [piece.reshape(3, 4, 128, 256) for piece in pieces]

    result, g1_own, grads_two, grads_proj, grads_one, small_grads, pixel_grad, part, psum = layers(
        where, blend, both_rows, vecs, idk, idr, pixels[0], pl_low, folded, pgain, segb, small_four,
        (*group_one, *group_proj, *group_two),
        (*halves(face_one, near_one), *halves(face_proj, near_proj), *halves(face_two, near_two)),
    )
    small_two, small_proj, small_one = small_grads[:8], small_grads[8:16], small_grads[16:]

    parts = []
    for k in range(4):
        third = lax.dynamic_slice(grads_proj, (0, (own ^ k) * 768), (64, 768))
        thirds = [third[:, 256 * j : 256 * j + 256] for j in range(3)]
        at = (0, (own ^ k) * 256)
        parts.append(
            jnp.concatenate(
                [lax.dynamic_slice(grads_two, at, (192, 256)), *thirds, lax.dynamic_slice(grads_one, at, (224, 256))], 0
            )
        )
    got_core = with_core(parts)

    sums = jnp.stack(in_three(psum)).reshape(6, channels)
    sent = jnp.concatenate(
        [
            part.reshape(32, 16, channels),
            jnp.broadcast_to(sums[None], (32, 6, channels)),
        ],
        1,
    )
    got = jnp.sum(lax.all_to_all(sent, CTX, 0, 0, tiled=True).astype(F32), 0)
    pixel_sums = (got[16:18] + got[18:20]) + got[20:22]
    near, far = with_facing(parts, got_core)
    total = (near + far.astype(F32)).astype(BF)
    first, second = paired(total[:320], "x"), paired(total[320:], "y")
    own_folded = after(got[:16].astype(BF), first, second)
    beside = [shift(first, "y", 1), shift(first, "y", 3), shift(second, "x", 1), shift(second, "x", 3)]
    folded_grad = after(spread(own_folded), beside)
    far_first, far_second = after((first, second), folded_grad)
    first = [first, beside[0], shift(far_first, "y", 2), beside[1]]
    second = [second, beside[2], shift(far_second, "x", 2), beside[3]]
    latent_total, late, small_zero = finish(
        where, folded_grad, both_rows, vecs, tcross, query, g1_own, query_four, small_four
    )
    small = jnp.stack(
        [
            *(small_zero[0], small_one[0], small_proj[0], small_two[0]),
            *(small_zero[1], small_one[1], small_proj[1], small_two[1]),
            *(small_one[2], small_one[3], small_two[2], small_two[3]),
        ]
    ).astype(BF)

    def sixfold(value):
        parts = jnp.pad(jnp.concatenate(in_three(value), 0), ((0, 0), (0, 512 - channels)))
        return parts.reshape(12, 256)

    def whole(parts):
        return jnp.sum(parts.reshape(3, 2, 512).astype(F32), 0)[:, :channels]

    small_parts = true_parts(small, own)
    parts = [
        jnp.concatenate([late[:, 256 * k : 256 * k + 256], small_parts[k]], 0) for k in range(4)
    ]
    got = lax.ppermute(
        jnp.concatenate([parts[1], parts[3], sixfold(pixel_sums)], 0), SHARD, [(i, i ^ 1) for i in range(4)]
    )
    near = parts[0].astype(F32) + got[:60].astype(F32)
    far = parts[2].astype(F32) + got[60:120].astype(F32)
    pixel_sums = pixel_sums + whole(got[120:])
    got = lax.ppermute(
        jnp.concatenate([far.astype(BF), sixfold(pixel_sums)], 0), SHARD, [(i, i ^ 2) for i in range(4)]
    )
    late_sum = near + got[:60].astype(F32)
    norm_part = late_sum[48:60]
    pix = pixel_sums + whole(got[60:])

    last = spread(late_sum[:48].astype(BF)).reshape(32, 48, 256)
    tall, few = (1024, 256), (channels, 256)
    bits = (0, 1, 3, 2)
    q, k = settle(
        where,
        [last],
        [[(0, 0, 32), (1, 0, 16)]],
        [tall, few],
        [[(0, (c,), lambda where, at=c: at) for c in range(32)]],
    )
    su, sd, so, proj, cu, cd, co, v = settle(
        after(where, q),
        [*first, *second],
        [
            [(0, 0, 64), (1, 0, 64), (2, 0, 64), (3, 0, 64), (3, 256, 64)],
            [(3, 512, 64), (4, 0, 64), (5, 0, 64), (6, 0, 64), (7, 0, 32)],
        ],
        [tall, tall, tall, (1024, 768), tall, tall, tall, few],
        [
            [(k, (b,), lambda where, k=k, b=b: (where[5] ^ bits[b]) * 4 + where[9 + k]) for k in range(4) for b in range(4)],
            [(4 + k, (b,), lambda where, k=k, b=b: where[5 + k] * 4 + (where[9] ^ bits[b])) for k in range(4) for b in range(4)],
        ],
    )
    return (
        result[None],
        latent_total[None],
        pixel_grad[None],
        pix[0],
        pix[1],
        q,
        k,
        v,
        co,
        cu,
        cd,
        proj,
        so,
        su,
        sd,
        norm_part[:4],
        norm_part[4:8],
        norm_part[8:12],
    )


def solution(mesh):
    fine = Mesh(mesh.devices.reshape(4, 2, 4, 2, 2), CTX + SHARD)
    rows = P(SHARD, CTX, None)
    cols = P(None, SHARD)
    return jax.shard_map(
        on_device,
        mesh=fine,
        in_specs=(
            rows,
            rows,
            P(SHARD, CTX),
            P(SHARD, None),
            P(),
            P(),
            *([cols] * 13),
            rows,
        ),
        out_specs=(rows, rows, rows, P(), P(), *([cols] * 13)),
        check_vma=False,
    )
```
